256 devices in a mesh: wide: 32 (over x, z_hi, y), narrow: 8 (over z_lo, core).
Axes of the slice: x: 4, y: 4, z: 8 (z_hi: 2, z_lo: 4; z = z_hi * 4 + z_lo), core: 2. Of those that a mesh axis runs over, the one named last changes fastest.
Arguments:
- amplitudes: bfloat16 [65536, 1024], P('wide', 'narrow'), may hold values from -6 to 6
- pair_mask: int32 [512, 8], P('wide', 'narrow'), may hold values 0 or 1
- integrals: bfloat16 [1024, 16384], P('wide', 'narrow'), may hold values from -0.1875 to 0.1875
Outputs:
- ladder: bfloat16 [65536, 16384], P('wide', 'narrow')
The draws below stay inside these ranges and needn't reach their ends.
All inputs are finite; a program needn't handle non-finite values. No bound on the sum of `pair_mask` on one device may be relied on, other than what follows from the above.
Results may differ from the reference program's by a relative error of at most 0.001.
Values may be sent and summed in bfloat16 or wider, within the bound.
A program may use at most 64 MiB of HBM per device.

```python
import jax
import jax.numpy as jnp
from jax import lax

VB = 128
KBLK = 8
KV = 1024
PAIRS = 65536
NV = 16384
PBLK = 512


def with_ends(entries, rng, smallest, high):
    longest = entries.shape.index(max(entries.shape))
    spots = []
    for shift in (0, 1):
        where = [jax.random.randint(jax.random.fold_in(rng, axis), (), 0, length) for axis, length in enumerate(entries.shape)]
        where[longest] = (where[longest] + shift) % entries.shape[longest]
        spots.append(tuple(where))
    return entries.at[spots[0]].set(smallest).at[spots[1]].set(high)


def block_scale(stream_key, shape, pieces, low, top_value):
    factor_of = 1.0
    for axis_at, blocks in pieces:
        draws = jax.random.uniform(jax.random.fold_in(jax.random.fold_in(stream_key, 6), axis_at), (blocks,), jnp.float32, low / len(pieces), top_value / len(pieces))
        factor_of = factor_of * jnp.repeat(jnp.exp(draws), shape[axis_at] // blocks).reshape((-1,) + (1,) * (len(shape) - 1 - axis_at))
    return factor_of


def bell_draw(stream_key, shape, width, reach, split=(), dtype=jnp.bfloat16):
    loudness = block_scale(stream_key, shape, split, -0.22, 0.18) if split else 1.0
    entries = jax.random.normal(stream_key, shape, jnp.float32) * width * loudness
    return jnp.minimum(jnp.maximum(entries, -reach), reach).astype(dtype)


def setup_inputs(seed: int = 0) -> dict:
    splits = jax.random.split(jax.random.key(seed), 4)
    return {
        "amplitudes": bell_draw(splits[0], (PAIRS, KV), 1.0, 6.0, ((0, 32), (1, 8))),
        "pair_mask": with_ends((jax.random.randint(splits[1], (PBLK, KBLK), 0, 2) < 1).astype(jnp.int32), jax.random.fold_in(splits[1], 1), 0, 1),
        "integrals": bell_draw(splits[2], (KV, NV), KV ** -0.5, 0.1875, ((0, 32), (1, 8))),
    }


def reference(amplitudes, pair_mask, integrals):
    tiles = jnp.repeat(jnp.repeat(pair_mask, VB, axis=0), VB, axis=1)
    masked = amplitudes * tiles.astype(jnp.bfloat16)
    blocks = masked.reshape(PBLK, VB, KV)

    def one_block(rows):
        return jnp.dot(rows, integrals, preferred_element_type=jnp.float32).astype(jnp.bfloat16)

    out = lax.map(one_block, blocks)
    return out.reshape(PAIRS, NV)
```

```python
import functools

import jax
import jax.numpy as jnp
from jax import lax
from jax.experimental import pallas as pl
from jax.experimental.pallas import tpu as pltpu
from jax.sharding import PartitionSpec as P

MESH = pl.DeviceIdType.MESH
VB = 128
LINE = 4
RING = 4
CORES = 2
CHUNK = 128
COLS = 512
WRITES = 8


def kernel(mask_ref, a_ref, b_ref, out_ref, a_in, a_all, b_all, local, za, ca, up, down, side, zb, sb):
    wide, narrow = lax.axis_index("wide"), lax.axis_index("narrow")
    zl, core = narrow // CORES, narrow % CORES
    x, zh, y = wide // (2 * RING), (wide // RING) % 2, wide % RING
    rows, width = a_in.shape
    depth = b_ref.shape[0]
    half = depth // 2
    chunks = rows // CHUNK

    def wide_of(layer, first, second):
        px = (x + (1 - core) * first + core * second) % RING
        py = (y + core * first + (1 - core) * second) % RING
        return (px * 2 + (zh + layer) % 2) * RING + py

    other = (wide, zl * CORES + 1 - core)
    above, below = (wide, narrow + CORES), (wide, narrow - CORES)

    take_b = pltpu.make_async_copy(b_ref, b_all.at[pl.ds(wide * depth, depth)], local.at[0])
    take_a = pltpu.make_async_copy(a_ref, a_in, local.at[1])
    take_b.start()
    take_a.start()

    barrier = pltpu.get_barrier_semaphore()

    def greet(device):
        pl.semaphore_signal(barrier, inc=1, device_id=device, device_id_type=MESH)

    for first, second in ((1, 0), (3, 0), (0, 1), (0, 3)):
        greet((wide_of(0, first, second), narrow))
    greet((wide_of(1, 0, 0), narrow))
    greet(other)

    @pl.when(zl < LINE - 1)
    def _():
        greet(above)

    @pl.when(zl > 0)
    def _():
        greet(below)

    inner = jnp.where((zl > 0) & (zl < LINE - 1), 1, 0)
    pl.semaphore_wait(barrier, 7 + inner)
    take_b.wait()

    sent = []

    def b_part(layer, first, second, part):
        base = wide_of(layer, first, second) * depth
        if part is None:
            return b_all.at[pl.ds(base, depth)]
        return b_all.at[pl.ds(base + part * half, half)]

    def b_copy(layer, first, second, part, to, label):
        where = b_part(layer, first, second, part)
        return pltpu.make_async_remote_copy(
            where,
            where,
            sb.at[len(sent)],
            zb.at[label[0], label[1] % RING, label[2] % RING, part or 0],
            device_id=(wide_of(*to), narrow),
            device_id_type=MESH,
        )

    def b_send(layer, first, second, part, step):
        df, ds = step
        copy = b_copy(layer, first, second, part, (0, df, ds), (layer, first - df, second - ds))
        copy.start()
        sent.append(copy)

    def b_wait(layer, first, second, part):
        where = b_part(layer, first, second, part)
        pltpu.make_async_remote_copy(
            where,
            where,
            sb.at[0],
            zb.at[layer, first % RING, second % RING, part or 0],
            device_id=other,
            device_id_type=MESH,
        ).wait_recv()

    def b_begin(layer):
        for step in ((1, 0), (3, 0), (0, 1), (0, 3)):
            b_send(layer, 0, 0, None, step)

    def b_near(layer):
        b_wait(layer, 3, 0, None)
        b_send(layer, 3, 0, 0, (1, 0))
        b_send(layer, 3, 0, None, (0, 1))
        b_send(layer, 3, 0, None, (0, 3))
        b_wait(layer, 1, 0, None)
        b_send(layer, 1, 0, 1, (3, 0))
        b_send(layer, 1, 0, None, (0, 1))
        b_send(layer, 1, 0, None, (0, 3))

    def b_far(layer):
        b_wait(layer, 2, 0, 0)
        b_wait(layer, 2, 0, 1)
        b_send(layer, 2, 0, None, (0, 1))
        b_send(layer, 2, 0, None, (0, 3))

    def b_turn(layer, first):
        b_wait(layer, first, 3, None)
        b_send(layer, first, 3, 0, (0, 1))
        b_wait(layer, first, 1, None)
        b_send(layer, first, 1, 1, (0, 3))

    def b_end(layer):
        for first in range(RING):
            b_wait(layer, first, 2, 0)
            b_wait(layer, first, 2, 1)

    swap = b_copy(0, 0, 0, None, (1, 0, 0), (1, 0, 0))
    swap.start()
    sent.append(swap)
    b_begin(0)

    def a_copy(source, r, send, recv, device):
        where = a_all.at[source, core, pl.ds(pl.multiple_of(r * CHUNK, CHUNK), CHUNK)]
        return pltpu.make_async_remote_copy(
            where, where, send.at[source, r], recv.at[source, r], device_id=device, device_id_type=MESH
        )

    def over(source, r):
        return a_copy(source, r, side, ca, other)

    def upward(source, r):
        return a_copy(source, r, up, za, above)

    def downward(source, r):
        return a_copy(source, r, down, za, below)

    def from_other(source, r):
        where = a_all.at[source, 1 - core, pl.ds(pl.multiple_of(r * CHUNK, CHUNK), CHUNK)]
        pltpu.make_async_remote_copy(
            where, where, side.at[source, r], ca.at[source, r], device_id=other, device_id_type=MESH
        ).wait_recv()

    take_a.wait()

    def own(r, _):
        span = pl.ds(pl.multiple_of(r * CHUNK, CHUNK), CHUNK)
        keep = mask_ref[0, r * CHUNK // VB].astype(jnp.float32)
        a_all[zl, core, span, :] = (a_in[span, :].astype(jnp.float32) * keep).astype(jnp.bfloat16)

        @pl.when(zl < LINE - 1)
        def _():
            upward(zl, r).start()

        @pl.when(zl > 0)
        def _():
            downward(zl, r).start()

        over(zl, r).start()
        return 0

    lax.fori_loop(0, chunks, own, 0)

    def forward(distance, r):
        @pl.when(zl - distance >= 0)
        def _():
            upward(zl - distance, r).wait_recv()

            @pl.when(zl < LINE - 1)
            def _():
                upward(zl - distance, r).start()

            over(zl - distance, r).start()

        @pl.when(zl + distance < LINE)
        def _():
            downward(zl + distance, r).wait_recv()

            @pl.when(zl > 0)
            def _():
                downward(zl + distance, r).start()

            over(zl + distance, r).start()

    def forwards(distance, start, stop):
        def body(r, _):
            forward(distance, r)
            return 0

        lax.fori_loop(start * chunks // 16, stop * chunks // 16, body, 0)

    b_near(0)
    b_far(0)
    for first in range(RING):
        b_turn(0, first)
    forwards(1, 0, 8)
    b_wait(1, 0, 0, None)
    b_begin(1)
    forwards(1, 8, 10)
    b_near(1)
    forwards(1, 10, 12)
    b_far(1)
    forwards(1, 12, 16)
    for first in range(RING):
        b_turn(1, first)
    b_end(0)
    b_end(1)
    forwards(2, 0, 16)

    def product(r):
        span = pl.ds(pl.multiple_of(r * CHUNK, CHUNK), CHUNK)
        for source in range(LINE):
            from_other(source, r)
        left = jnp.concatenate([a_all[s, c, span, :] for s in range(LINE) for c in range(CORES)], axis=1)
        for start in range(0, out_ref.shape[1], COLS):
            out_ref[span, start : start + COLS] = jnp.dot(
                left, b_all[:, start : start + COLS], preferred_element_type=jnp.float32
            ).astype(out_ref.dtype)

    def last(r, _):
        forward(3, r)

        @pl.when(r > 0)
        def _():
            product(r - 1)

        return 0

    lax.fori_loop(0, chunks, last, 0)
    product(chunks - 1)

    for copy in sent:
        copy.wait_send()

    def finish(i, _):
        source, r = i // chunks, i % chunks
        over(source, r).wait_send()

        @pl.when((source <= zl) & (zl < LINE - 1))
        def _():
            upward(source, r).wait_send()

        @pl.when((source >= zl) & (zl > 0))
        def _():
            downward(source, r).wait_send()

        return 0

    lax.fori_loop(0, LINE * chunks, finish, 0)


def write_out(from_ref, to_ref, sem):
    size = from_ref.shape[0] // WRITES
    copies = [
        pltpu.make_async_copy(from_ref.at[pl.ds(i * size, size)], to_ref.at[pl.ds(i * size, size)], sem.at[i])
        for i in range(WRITES)
    ]
    for copy in copies:
        copy.start()
    for copy in copies:
        copy.wait()


def shards(amplitudes, pair_mask, integrals):
    rows, width = amplitudes.shape
    depth, columns = integrals.shape
    deep = depth * 2 * RING * RING
    chunks = rows // CHUNK
    dma = pltpu.SemaphoreType.DMA
    result = pl.pallas_call(
        kernel,
        out_shape=jax.ShapeDtypeStruct((rows, columns), jnp.bfloat16),
        in_specs=[
            pl.BlockSpec(memory_space=pltpu.SMEM),
            pl.BlockSpec(memory_space=pltpu.HBM),
            pl.BlockSpec(memory_space=pltpu.HBM),
        ],
        out_specs=pl.BlockSpec(memory_space=pltpu.VMEM),
        scratch_shapes=[
            pltpu.VMEM((rows, width), jnp.bfloat16),
            pltpu.VMEM((LINE, CORES, rows, width), jnp.bfloat16),
            pltpu.VMEM((deep, columns), jnp.bfloat16),
            dma((2,)),
            dma((LINE, chunks)),
            dma((LINE, chunks)),
            dma((LINE, chunks)),
            dma((LINE, chunks)),
            dma((LINE, chunks)),
            dma((2, RING, RING, 2)),
            dma((48,)),
        ],
        compiler_params=pltpu.CompilerParams(
            collective_id=0, has_side_effects=True, vmem_limit_bytes=32 * 2**20
        ),
        cost_estimate=pl.CostEstimate(
            flops=2 * rows * columns * deep, bytes_accessed=2 * rows * columns, transcendentals=0
        ),
    )(pair_mask.reshape(1, -1), amplitudes, integrals)
    return pl.pallas_call(
        write_out,
        out_shape=jax.ShapeDtypeStruct(result.shape, result.dtype),
        in_specs=[pl.BlockSpec(memory_space=pl.ANY)],
        out_specs=pl.BlockSpec(memory_space=pltpu.HBM),
        scratch_shapes=[dma((WRITES,))],
        compiler_params=pltpu.CompilerParams(vmem_limit_bytes=2**20),
        cost_estimate=pl.CostEstimate(flops=0, bytes_accessed=2 * rows * columns, transcendentals=0),
    )(result)


def solution(mesh):
    placed = P("wide", "narrow")
    return jax.shard_map(
        shards, mesh=mesh, in_specs=(placed, placed, placed), out_specs=placed, check_vma=False
    )
```

```python
import functools

import jax
import jax.numpy as jnp
from jax import lax
from jax.experimental import pallas as pl
from jax.experimental.pallas import tpu as pltpu
from jax.sharding import PartitionSpec as P

MESH = pl.DeviceIdType.MESH
VB = 128
LINE = 4
RING = 4
CORES = 2
CHUNK = 128
BLOCK = 256
TALL = 512
COLS = 512
WRITES = 8


def kernel(
    mask_hbm, a_ref, b_ref, out_ref, mask_ref, a_in, a_all, b_all, total, local, za, ca, up, down, side, zb, sb, ready
):
    wide, narrow = lax.axis_index("wide"), lax.axis_index("narrow")
    zl, core = narrow // CORES, narrow % CORES
    x, zh, y = wide // (2 * RING), (wide // RING) % 2, wide % RING
    rows, width = a_in.shape
    depth = b_ref.shape[0]
    half = depth // 2
    chunks = rows // CHUNK
    near = jnp.where(zl < LINE // 2, 0, LINE // 2)
    middle = jnp.where(zl < LINE // 2, LINE // 2, LINE // 2 - 1)
    late = jnp.where(zl < LINE // 2, LINE - 1, 0)

    def wide_of(layer, first, second):
        px = (x + (1 - core) * first + core * second) % RING
        py = (y + core * first + (1 - core) * second) % RING
        return (px * 2 + (zh + layer) % 2) * RING + py

    other = (wide, zl * CORES + 1 - core)
    above, below = (wide, narrow + CORES), (wide, narrow - CORES)

    take_b = pltpu.make_async_copy(b_ref, b_all.at[pl.ds(wide * depth, depth)], local.at[0])
    take_a = pltpu.make_async_copy(a_ref, a_in, local.at[1])
    take_mask = pltpu.make_async_copy(mask_hbm, mask_ref, local.at[2])
    take_a.start()
    take_mask.start()
    take_b.start()

    barrier = pltpu.get_barrier_semaphore()

    def greet(device):
        pl.semaphore_signal(barrier, inc=1, device_id=device, device_id_type=MESH)

    for first, second in ((1, 0), (3, 0), (0, 1), (0, 3)):
        greet((wide_of(0, first, second), narrow))
    greet(other)
    peer = (wide_of(1, 0, 0), narrow)

    @pl.when(zh == 0)
    def _():
        greet(peer)

    @pl.when(zl < LINE - 1)
    def _():
        greet(above)

    @pl.when(zl > 0)
    def _():
        greet(below)

    inner = jnp.where((zl > 0) & (zl < LINE - 1), 1, 0)
    pl.semaphore_wait(barrier, 6 + inner + zh)


    def b_part(layer, first, second, part):
        base = wide_of(layer, first, second) * depth
        if part is None:
            return b_all.at[pl.ds(base, depth)]
        return b_all.at[pl.ds(base + part * half, half)]

    def b_copy(layer, first, second, part, to, label):
        where = b_part(layer, first, second, part)
        return pltpu.make_async_remote_copy(
            where,
            where,
            sb.at[0],
            zb.at[label[0], label[1] % RING, label[2] % RING, part or 0],
            device_id=(wide_of(*to), narrow),
            device_id_type=MESH,
        )

    def b_send(layer, first, second, part, step):
        df, ds = step
        b_copy(layer, first, second, part, (0, df, ds), (layer, first - df, second - ds)).start()

    def b_wait(layer, first, second, part):
        where = b_part(layer, first, second, part)
        pltpu.make_async_remote_copy(
            where,
            where,
            sb.at[0],
            zb.at[layer, first % RING, second % RING, part or 0],
            device_id=other,
            device_id_type=MESH,
        ).wait_recv()

    def b_begin(layer):
        for step in ((1, 0), (3, 0), (0, 1), (0, 3)):
            b_send(layer, 0, 0, None, step)

    def b_near(layer):
        b_wait(layer, 3, 0, None)
        b_send(layer, 3, 0, 0, (1, 0))
        b_send(layer, 3, 0, None, (0, 1))
        b_send(layer, 3, 0, None, (0, 3))
        b_wait(layer, 1, 0, None)
        b_send(layer, 1, 0, 1, (3, 0))
        b_send(layer, 1, 0, None, (0, 1))
        b_send(layer, 1, 0, None, (0, 3))

    def b_far(layer):
        b_wait(layer, 2, 0, 0)
        b_wait(layer, 2, 0, 1)
        b_send(layer, 2, 0, None, (0, 1))
        b_send(layer, 2, 0, None, (0, 3))

    def b_turn(layer, first):
        b_wait(layer, first, 3, None)
        b_send(layer, first, 3, 0, (0, 1))
        b_wait(layer, first, 1, None)
        b_send(layer, first, 1, 1, (0, 3))

    def b_end(layer):
        for first in range(RING):
            b_wait(layer, first, 2, 0)
            b_wait(layer, first, 2, 1)

    swap = b_copy(0, 0, 0, None, (1, 0, 0), (1, 0, 0))
    take_b.wait()

    @pl.when(zh == 1)
    def _():
        pl.semaphore_signal(ready, inc=1, device_id=peer, device_id_type=MESH)
        swap.start()

    def a_copy(source, r, send, recv, device):
        where = a_all.at[source, core, pl.ds(pl.multiple_of(r * CHUNK, CHUNK), CHUNK)]
        return pltpu.make_async_remote_copy(
            where, where, send.at[source], recv, device_id=device, device_id_type=MESH
        )

    def over(source, r):
        return a_copy(source, r, side, ca.at[source, jnp.where(source == late, r, 0)], other)

    def upward(source, r):
        return a_copy(source, r, up, za.at[source, r], above)

    def downward(source, r):
        return a_copy(source, r, down, za.at[source, r], below)

    def from_other(where, r, source):
        pltpu.make_async_remote_copy(
            where, where, side.at[source], ca.at[source, r], device_id=other, device_id_type=MESH
        ).wait_recv()

    take_a.wait()
    take_mask.wait()

    def own(r, _):
        span = pl.ds(pl.multiple_of(r * CHUNK, CHUNK), CHUNK)
        keep = mask_ref[0, r * CHUNK // VB].astype(jnp.float32)
        a_all[zl, core, span, :] = (a_in[span, :].astype(jnp.float32) * keep).astype(jnp.bfloat16)

        @pl.when(zl < LINE - 1)
        def _():
            upward(zl, r).start()

        @pl.when(zl > 0)
        def _():
            downward(zl, r).start()

        over(zl, r).start()
        return 0

    lax.fori_loop(0, chunks, own, 0)

    def forward(distance, r):
        @pl.when(zl - distance >= 0)
        def _():
            upward(zl - distance, r).wait_recv()

            @pl.when(zl < LINE - 1)
            def _():
                upward(zl - distance, r).start()

            over(zl - distance, r).start()

        @pl.when(zl + distance < LINE)
        def _():
            downward(zl + distance, r).wait_recv()

            @pl.when(zl > 0)
            def _():
                downward(zl + distance, r).start()

            over(zl + distance, r).start()

    def forwards(distance, start, stop):
        def body(r, _):
            forward(distance, r)
            return 0

        lax.fori_loop(start * chunks // 16, stop * chunks // 16, body, 0)

    def tile(place, c, span):
        return a_all[place, c, span, :]

    def deep(place, c):
        return pl.ds(pl.multiple_of((place * CORES + c) * width, width), width)

    def multiply(places, span, start):
        left = jnp.concatenate([tile(place, c, span) for place, c in places], axis=1)
        right = jnp.concatenate([b_all[deep(place, c), start : start + COLS] for place, c in places], axis=0)
        return jnp.dot(left, right, preferred_element_type=jnp.float32)

    def first_part(q):
        span = pl.ds(pl.multiple_of(q * TALL, TALL), TALL)
        for start in range(0, out_ref.shape[1], COLS):
            total[span, start : start + COLS] = multiply([(near, zh), (near + 1, zh)], span, start)

    def second_part(q):
        span = pl.ds(pl.multiple_of(q * TALL, TALL), TALL)
        places = [(near, 1 - zh), (near + 1, 1 - zh), (middle, 0), (middle, 1)]
        for start in range(0, out_ref.shape[1], COLS):
            total[span, start : start + COLS] += multiply(places, span, start)

    talls = rows // TALL

    def first_parts(start, stop):
        first_chunk, last_chunk = start, stop

        def body(q, _):
            first_part(q)
            per = (last_chunk - first_chunk) // talls
            for i in range(per):
                forward(2, first_chunk + q * per + i)
            return 0

        lax.fori_loop(0, talls, body, 0)

    def second_parts():
        per = chunks // 2 // talls

        def body(q, _):
            second_part(q)
            for i in range(per):
                forward(3, q * per + i)
            return 0

        lax.fori_loop(0, talls, body, 0)

    b_begin(0)
    b_near(0)
    b_turn(0, 0)

    @pl.when(zh == 0)
    def _():
        pl.semaphore_wait(ready, 1)
        swap.start()

    b_far(0)
    b_turn(0, 3)
    forwards(1, 0, 6)
    b_turn(0, 1)
    forwards(1, 6, 10)
    b_turn(0, 2)
    forwards(1, 10, 14)
    b_wait(1, 0, 0, None)
    b_begin(1)
    forwards(1, 14, 16)
    b_near(1)
    b_turn(1, 0)
    forwards(2, 0, 2)
    b_far(1)
    b_turn(1, 3)
    forwards(2, 2, 5)
    b_turn(1, 1)
    forwards(2, 5, 8)
    b_turn(1, 2)
    b_end(0)
    for i in range(2):
        from_other(a_all.at[near + i, 1 - core], 0, near + i)
    first_parts(8, 16)
    b_end(1)
    from_other(a_all.at[middle, 1 - core], 0, middle)
    second_parts()

    def final(q):
        for i in range(BLOCK // CHUNK):
            r = q * (BLOCK // CHUNK) + i
            from_other(a_all.at[late, 1 - core, pl.ds(pl.multiple_of(r * CHUNK, CHUNK), CHUNK)], r, late)
        span = pl.ds(pl.multiple_of(q * BLOCK, BLOCK), BLOCK)
        for start in range(0, out_ref.shape[1], COLS):
            out_ref[span, start : start + COLS] = (
                total[span, start : start + COLS] + multiply([(late, 0), (late, 1)], span, start)
            ).astype(out_ref.dtype)

    blocks = rows // BLOCK

    def last_part(r, _):
        for i in range(chunks // 2 // blocks):
            forward(3, chunks // 2 + r * (chunks // 2 // blocks) + i)
        final(r)
        return 0

    lax.fori_loop(0, blocks, last_part, 0)

    everything = b_all.at[pl.ds(0, b_all.shape[0] - depth)]
    pltpu.make_async_remote_copy(
        everything, everything, sb.at[0], zb.at[0, 0, 0, 0], device_id=other, device_id_type=MESH
    ).wait_send()

    def finish(source, _):
        def sent(sem):
            where = a_all.at[source, core]
            pltpu.make_async_remote_copy(
                where, where, sem.at[source], za.at[0, 0], device_id=other, device_id_type=MESH
            ).wait_send()

        sent(side)

        @pl.when((source <= zl) & (zl < LINE - 1))
        def _():
            sent(up)

        @pl.when((source >= zl) & (zl > 0))
        def _():
            sent(down)

        return 0

    lax.fori_loop(0, LINE, finish, 0)


def write_out(from_ref, to_ref, sem):
    size = from_ref.shape[0] // WRITES
    copies = [
        pltpu.make_async_copy(from_ref.at[pl.ds(i * size, size)], to_ref.at[pl.ds(i * size, size)], sem.at[i])
        for i in range(WRITES)
    ]
    for copy in copies:
        copy.start()
    for copy in copies:
        copy.wait()


def shards(amplitudes, pair_mask, integrals):
    rows, width = amplitudes.shape
    depth, columns = integrals.shape
    deep = depth * 2 * RING * RING
    chunks = rows // CHUNK
    dma = pltpu.SemaphoreType.DMA
    result = pl.pallas_call(
        kernel,
        out_shape=jax.ShapeDtypeStruct((rows, columns), jnp.bfloat16),
        in_specs=[
            pl.BlockSpec(memory_space=pltpu.HBM),
            pl.BlockSpec(memory_space=pltpu.HBM),
            pl.BlockSpec(memory_space=pltpu.HBM),
        ],
        out_specs=pl.BlockSpec(memory_space=pltpu.VMEM),
        scratch_shapes=[
            pltpu.SMEM((1, rows // VB), jnp.int32),
            pltpu.VMEM((rows, width), jnp.bfloat16),
            pltpu.VMEM((LINE, CORES, rows, width), jnp.bfloat16),
            pltpu.VMEM((deep, columns), jnp.bfloat16),
            pltpu.VMEM((rows, columns), jnp.float32),
            dma((3,)),
            dma((LINE, chunks)),
            dma((LINE, chunks)),
            dma((LINE,)),
            dma((LINE,)),
            dma((LINE,)),
            dma((2, RING, RING, 2)),
            dma((1,)),
            pltpu.SemaphoreType.REGULAR,
        ],
        compiler_params=pltpu.CompilerParams(
            collective_id=0, has_side_effects=True, vmem_limit_bytes=40 * 2**20
        ),
        cost_estimate=pl.CostEstimate(
            flops=2 * rows * columns * deep, bytes_accessed=2 * rows * columns, transcendentals=0
        ),
    )(*[pltpu.with_memory_space_constraint(v, pltpu.HBM) for v in (pair_mask.reshape(1, -1), amplitudes, integrals)])
    return pl.pallas_call(
        write_out,
        out_shape=jax.ShapeDtypeStruct(result.shape, result.dtype),
        in_specs=[pl.BlockSpec(memory_space=pl.ANY)],
        out_specs=pl.BlockSpec(memory_space=pltpu.HBM),
        scratch_shapes=[dma((WRITES,))],
        compiler_params=pltpu.CompilerParams(vmem_limit_bytes=2**20),
        cost_estimate=pl.CostEstimate(flops=0, bytes_accessed=2 * rows * columns, transcendentals=0),
    )(result)


def solution(mesh):
    placed = P("wide", "narrow")
    return jax.shard_map(
        shards, mesh=mesh, in_specs=(placed, placed, placed), out_specs=placed, check_vma=False
    )
```

```python
import functools

import jax
import jax.numpy as jnp
from jax import lax
from jax.experimental import pallas as pl
from jax.experimental.pallas import tpu as pltpu
from jax.sharding import PartitionSpec as P

MESH = pl.DeviceIdType.MESH
VB = 128
LINE = 4
RING = 4
CORES = 2
CHUNK = 128
BLOCK = 256
TALL = 512
REST = 512
COLS = 512


def kernel(
    mask_hbm,
    a_ref,
    b_ref,
    out_ref,
    total_rest,
    a_rest,
    b_rest,
    mask_ref,
    a_in,
    a_all,
    b_all,
    total,
    local,
    za,
    ca,
    up,
    down,
    side,
    zb,
    sb,
    ready,
):
    wide, narrow = lax.axis_index("wide"), lax.axis_index("narrow")
    zl, core = narrow // CORES, narrow % CORES
    x, zh, y = wide // (2 * RING), (wide // RING) % 2, wide % RING
    rows, width = a_in.shape
    depth = b_ref.shape[0]
    half = depth // 2
    chunks = rows // CHUNK
    near = jnp.where(zl < LINE // 2, 0, LINE // 2)
    middle = jnp.where(zl < LINE // 2, LINE // 2, LINE // 2 - 1)
    late = jnp.where(zl < LINE // 2, LINE - 1, 0)

    def wide_of(layer, first, second):
        px = (x + (1 - core) * first + core * second) % RING
        py = (y + core * first + (1 - core) * second) % RING
        return (px * 2 + (zh + layer) % 2) * RING + py

    other = (wide, zl * CORES + 1 - core)
    above, below = (wide, narrow + CORES), (wide, narrow - CORES)

    take_b = pltpu.make_async_copy(b_ref, b_all.at[pl.ds(wide * depth, depth)], local.at[0])
    take_a = pltpu.make_async_copy(a_ref, a_in, local.at[1])
    take_mask = pltpu.make_async_copy(mask_hbm, mask_ref, local.at[2])
    take_a.start()
    take_mask.start()
    take_b.start()

    barrier = pltpu.get_barrier_semaphore()

    def greet(device):
        pl.semaphore_signal(barrier, inc=1, device_id=device, device_id_type=MESH)

    for first, second in ((1, 0), (3, 0), (0, 1), (0, 3)):
        greet((wide_of(0, first, second), narrow))
    greet(other)
    peer = (wide_of(1, 0, 0), narrow)

    @pl.when(zh == 0)
    def _():
        greet(peer)

    @pl.when(zl < LINE - 1)
    def _():
        greet(above)

    @pl.when(zl > 0)
    def _():
        greet(below)

    inner = jnp.where((zl > 0) & (zl < LINE - 1), 1, 0)
    pl.semaphore_wait(barrier, 6 + inner + zh)


    def b_part(layer, first, second, part):
        base = wide_of(layer, first, second) * depth
        if part is None:
            return b_all.at[pl.ds(base, depth)]
        return b_all.at[pl.ds(base + part * half, half)]

    def b_copy(layer, first, second, part, to, label):
        where = b_part(layer, first, second, part)
        return pltpu.make_async_remote_copy(
            where,
            where,
            sb.at[0],
            zb.at[label[0], label[1] % RING, label[2] % RING, part or 0],
            device_id=(wide_of(*to), narrow),
            device_id_type=MESH,
        )

    def b_send(layer, first, second, part, step):
        df, ds = step
        b_copy(layer, first, second, part, (0, df, ds), (layer, first - df, second - ds)).start()

    def b_wait(layer, first, second, part):
        where = b_part(layer, first, second, part)
        pltpu.make_async_remote_copy(
            where,
            where,
            sb.at[0],
            zb.at[layer, first % RING, second % RING, part or 0],
            device_id=other,
            device_id_type=MESH,
        ).wait_recv()

    def b_both(layer, first, part):
        b_send(layer, first, 0, part, (0, 1))
        b_send(layer, first, 0, part, (0, 3))

    def b_begin(layer, part):
        b_send(layer, 0, 0, part, (1, 0))
        b_send(layer, 0, 0, part, (3, 0))
        b_both(layer, 0, part)

    def b_near(layer, part):
        ahead, behind = ((3, 1), (1, 3))[part]
        b_wait(layer, ahead, 0, part)
        b_send(layer, ahead, 0, part, (behind, 0))
        b_both(layer, ahead, part)
        b_wait(layer, behind, 0, part)
        b_both(layer, behind, part)

    def b_far(layer, part):
        b_wait(layer, 2, 0, part)
        b_both(layer, 2, part)

    def b_turn(layer, first):
        b_wait(layer, first, 3, 0)
        b_send(layer, first, 3, 0, (0, 1))
        b_wait(layer, first, 1, 1)
        b_send(layer, first, 1, 1, (0, 3))

    def b_end(layer):
        for first in range(RING):
            b_wait(layer, first, 3, 1)
            b_wait(layer, first, 1, 0)
            b_wait(layer, first, 2, 0)
            b_wait(layer, first, 2, 1)

    swaps = [b_copy(0, 0, 0, part, (1, 0, 0), (1, 0, 0)) for part in (0, 1)]
    take_b.wait()

    @pl.when(zh == 1)
    def _():
        pl.semaphore_signal(ready, inc=1, device_id=peer, device_id_type=MESH)
        for swap in swaps:
            swap.start()

    def a_copy(source, r, send, recv, device):
        where = a_all.at[source, core, pl.ds(pl.multiple_of(r * CHUNK, CHUNK), CHUNK)]
        return pltpu.make_async_remote_copy(
            where, where, send.at[source], recv, device_id=device, device_id_type=MESH
        )

    def over(source, r):
        return a_copy(source, r, side, ca.at[source, jnp.where(source == late, r, 0)], other)

    def upward(source, r):
        return a_copy(source, r, up, za.at[source, r], above)

    def downward(source, r):
        return a_copy(source, r, down, za.at[source, r], below)

    def from_other(where, r, source):
        pltpu.make_async_remote_copy(
            where, where, side.at[source], ca.at[source, r], device_id=other, device_id_type=MESH
        ).wait_recv()

    take_a.wait()
    take_mask.wait()

    def own(r, _):
        span = pl.ds(pl.multiple_of(r * CHUNK, CHUNK), CHUNK)
        keep = mask_ref[0, r * CHUNK // VB].astype(jnp.float32)
        a_all[zl, core, span, :] = (a_in[span, :].astype(jnp.float32) * keep).astype(jnp.bfloat16)

        @pl.when(zl < LINE - 1)
        def _():
            upward(zl, r).start()

        @pl.when(zl > 0)
        def _():
            downward(zl, r).start()

        over(zl, r).start()
        return 0

    b_begin(0, 0)
    b_begin(0, 1)
    lax.fori_loop(0, chunks, own, 0)

    def forward(distance, r):
        @pl.when(zl - distance >= 0)
        def _():
            upward(zl - distance, r).wait_recv()

            @pl.when(zl < LINE - 1)
            def _():
                upward(zl - distance, r).start()

            over(zl - distance, r).start()

        @pl.when(zl + distance < LINE)
        def _():
            downward(zl + distance, r).wait_recv()

            @pl.when(zl > 0)
            def _():
                downward(zl + distance, r).start()

            over(zl + distance, r).start()

    def forwards(distance, start, stop):
        def body(r, _):
            forward(distance, r)
            return 0

        lax.fori_loop(start * chunks // 16, stop * chunks // 16, body, 0)

    def tile(place, c, span):
        return a_all[place, c, span, :]

    def deep(place, c):
        return pl.ds(pl.multiple_of((place * CORES + c) * width, width), width)

    def multiply(places, span, start):
        left = jnp.concatenate([tile(place, c, span) for place, c in places], axis=1)
        right = jnp.concatenate([b_all[deep(place, c), start : start + COLS] for place, c in places], axis=0)
        return jnp.dot(left, right, preferred_element_type=jnp.float32)

    columns = out_ref.shape[1]
    talls = total.shape[0] // TALL
    rest_talls = REST // TALL

    def first_part(q, into, skip):
        span = pl.ds(pl.multiple_of((q + skip) * TALL, TALL), TALL)
        here = pl.ds(pl.multiple_of(q * TALL, TALL), TALL)
        for start in range(0, columns, COLS):
            into[here, start : start + COLS] = multiply([(near, zh), (near + 1, zh)], span, start)

    def second_part(q, into, skip):
        span = pl.ds(pl.multiple_of((q + skip) * TALL, TALL), TALL)
        here = pl.ds(pl.multiple_of(q * TALL, TALL), TALL)
        places = [(near, 1 - zh), (near + 1, 1 - zh), (middle, 0), (middle, 1)]
        for start in range(0, columns, COLS):
            into[here, start : start + COLS] += multiply(places, span, start)

    def parts(part, distance, first_chunk, last_chunk):
        per = (last_chunk - first_chunk) // (talls + rest_talls)

        def body(q, _):
            part(q, total, 0)
            for i in range(per):
                forward(distance, first_chunk + q * per + i)
            return 0

        def rest_body(q, _):
            part(q, total_rest, talls)
            for i in range(per):
                forward(distance, first_chunk + (talls + q) * per + i)
            return 0

        lax.fori_loop(0, talls, body, 0)
        lax.fori_loop(0, rest_talls, rest_body, 0)

    def slice_of(q):
        if q < talls:
            first_part(q, total, 0)
        else:
            first_part(q - talls, total_rest, talls)

    b_near(0, 0)
    b_near(0, 1)
    b_turn(0, 0)

    @pl.when(zh == 0)
    def _():
        pl.semaphore_wait(ready, 1)
        for swap in swaps:
            swap.start()

    b_far(0, 0)
    b_far(0, 1)
    b_turn(0, 3)
    forwards(1, 0, 6)
    b_turn(0, 1)
    forwards(1, 6, 10)
    b_turn(0, 2)
    forwards(1, 10, 12)
    b_wait(1, 0, 0, 0)
    b_begin(1, 0)
    forwards(1, 12, 14)
    b_wait(1, 0, 0, 1)
    b_begin(1, 1)
    b_near(1, 0)
    forwards(1, 14, 16)
    b_near(1, 1)
    b_end(0)
    for i in range(2):
        from_other(a_all.at[near + i, 1 - core], 0, near + i)
    b_far(1, 0)
    slice_of(0)
    b_turn(1, 0)
    b_far(1, 1)
    slice_of(1)
    forwards(2, 0, 2)
    b_turn(1, 3)
    slice_of(2)
    forwards(2, 2, 5)
    b_turn(1, 1)
    slice_of(3)
    forwards(2, 5, 8)
    b_turn(1, 2)
    forwards(2, 8, 16)
    b_end(1)
    from_other(a_all.at[middle, 1 - core], 0, middle)
    b_rest[...] = b_all[pl.ds(pl.multiple_of(late * CORES * width, CORES * width), CORES * width)]
    parts(second_part, 3, 0, 8)

    def arrive(start, stop):
        def body(r, _):
            from_other(a_all.at[late, 1 - core, pl.ds(pl.multiple_of(r * CHUNK, CHUNK), CHUNK)], r, late)
            return 0

        lax.fori_loop(start, stop, body, 0)

    def final(q):
        span = pl.ds(pl.multiple_of(q * BLOCK, BLOCK), BLOCK)
        for start in range(0, columns, COLS):
            out_ref[span, start : start + COLS] = (
                total[span, start : start + COLS] + multiply([(late, 0), (late, 1)], span, start)
            ).astype(out_ref.dtype)

    blocks = total.shape[0] // BLOCK
    per = BLOCK // CHUNK

    def last_part(q, _):
        forward(3, chunks // 2 + q)
        arrive(q * per, (q + 1) * per)
        final(q)
        return 0

    lax.fori_loop(0, blocks, last_part, 0)

    def last_forward(r, _):
        forward(3, r)
        return 0

    lax.fori_loop(chunks // 2 + blocks, chunks, last_forward, 0)
    arrive(blocks * per, chunks)
    for c in range(CORES):
        a_rest[:, c * width : (c + 1) * width] = a_all[late, c, pl.ds(rows - REST, REST), :]

    everything = b_all.at[pl.ds(0, b_all.shape[0] - depth)]
    pltpu.make_async_remote_copy(
        everything, everything, sb.at[0], zb.at[0, 0, 0, 0], device_id=other, device_id_type=MESH
    ).wait_send()

    def finish(source, _):
        def sent(sem):
            where = a_all.at[source, core]
            pltpu.make_async_remote_copy(
                where, where, sem.at[source], za.at[0, 0], device_id=other, device_id_type=MESH
            ).wait_send()

        sent(side)

        @pl.when((source <= zl) & (zl < LINE - 1))
        def _():
            sent(up)

        @pl.when((source >= zl) & (zl > 0))
        def _():
            sent(down)

        return 0

    lax.fori_loop(0, LINE, finish, 0)


def finish_rows(done_ref, total_ref, a_ref, b_ref, to_ref, last, sem):
    size, done = BLOCK, done_ref.shape[0]
    copies = []

    def send(where, row):
        copy = pltpu.make_async_copy(where, to_ref.at[pl.ds(row, size)], sem.at[len(copies)])
        copy.start()
        copies.append(copy)

    for row in range(0, done, size):
        send(done_ref.at[pl.ds(row, size)], row)
    for row in range(0, last.shape[0], size):
        for start in range(0, last.shape[1], COLS):
            last[row : row + size, start : start + COLS] = (
                total_ref[row : row + size, start : start + COLS]
                + jnp.dot(
                    a_ref[row : row + size], b_ref[:, start : start + COLS], preferred_element_type=jnp.float32
                )
            ).astype(last.dtype)
        send(last.at[pl.ds(row, size)], done + row)
    for copy in copies:
        copy.wait()


def shards(amplitudes, pair_mask, integrals):
    rows, width = amplitudes.shape
    depth, columns = integrals.shape
    deep = depth * 2 * RING * RING
    chunks = rows // CHUNK
    dma = pltpu.SemaphoreType.DMA
    held = pl.pallas_call(
        kernel,
        out_shape=[
            jax.ShapeDtypeStruct((rows - REST, columns), jnp.bfloat16),
            jax.ShapeDtypeStruct((REST, columns), jnp.float32),
            jax.ShapeDtypeStruct((REST, CORES * width), jnp.bfloat16),
            jax.ShapeDtypeStruct((CORES * width, columns), jnp.bfloat16),
        ],
        in_specs=[
            pl.BlockSpec(memory_space=pltpu.HBM),
            pl.BlockSpec(memory_space=pltpu.HBM),
            pl.BlockSpec(memory_space=pltpu.HBM),
        ],
        out_specs=[pl.BlockSpec(memory_space=pltpu.VMEM)] * 4,
        scratch_shapes=[
            pltpu.SMEM((1, rows // VB), jnp.int32),
            pltpu.VMEM((rows, width), jnp.bfloat16),
            pltpu.VMEM((LINE, CORES, rows, width), jnp.bfloat16),
            pltpu.VMEM((deep, columns), jnp.bfloat16),
            pltpu.VMEM((rows - REST, columns), jnp.float32),
            dma((3,)),
            dma((LINE, chunks)),
            dma((LINE, chunks)),
            dma((LINE,)),
            dma((LINE,)),
            dma((LINE,)),
            dma((2, RING, RING, 2)),
            dma((1,)),
            pltpu.SemaphoreType.REGULAR,
        ],
        compiler_params=pltpu.CompilerParams(
            collective_id=0, has_side_effects=True, vmem_limit_bytes=40 * 2**20
        ),
        cost_estimate=pl.CostEstimate(
            flops=2 * rows * columns * deep, bytes_accessed=2 * rows * columns, transcendentals=0
        ),
    )(*[pltpu.with_memory_space_constraint(v, pltpu.HBM) for v in (pair_mask.reshape(1, -1), amplitudes, integrals)])
    return pl.pallas_call(
        finish_rows,
        out_shape=jax.ShapeDtypeStruct((rows, columns), jnp.bfloat16),
        in_specs=[pl.BlockSpec(memory_space=pltpu.VMEM)] * 4,
        out_specs=pl.BlockSpec(memory_space=pltpu.HBM),
        scratch_shapes=[pltpu.VMEM((REST, columns), jnp.bfloat16), dma((rows // BLOCK,))],
        compiler_params=pltpu.CompilerParams(vmem_limit_bytes=20 * 2**20),
        cost_estimate=pl.CostEstimate(
            flops=2 * REST * columns * CORES * width, bytes_accessed=2 * rows * columns, transcendentals=0
        ),
    )(*held)


def solution(mesh):
    placed = P("wide", "narrow")
    return jax.shard_map(
        shards, mesh=mesh, in_specs=(placed, placed, placed), out_specs=placed, check_vma=False
    )
```

```python
import functools

import jax
import jax.numpy as jnp
from jax import lax
from jax.experimental import pallas as pl
from jax.experimental.pallas import tpu as pltpu
from jax.sharding import PartitionSpec as P

MESH = pl.DeviceIdType.MESH
VB = 128
LINE = 4
RING = 4
CORES = 2
CHUNK = 128
BLOCK = 256
TALL = 512
REST = 1024
AHEAD = 6
COLS = 512


def kernel(
    mask_hbm,
    a_ref,
    b_ref,
    out_ref,
    total_rest,
    a_rest,
    b_rest,
    mask_ref,
    a_in,
    a_all,
    b_all,
    total,
    local,
    za,
    ca,
    up,
    down,
    side,
    zb,
    sb,
    ready,
):
    wide, narrow = lax.axis_index("wide"), lax.axis_index("narrow")
    zl, core = narrow // CORES, narrow % CORES
    x, zh, y = wide // (2 * RING), (wide // RING) % 2, wide % RING
    rows, width = a_in.shape
    depth = b_ref.shape[0]
    half = depth // 2
    chunks = rows // CHUNK
    near = jnp.where(zl < LINE // 2, 0, LINE // 2)
    middle = jnp.where(zl < LINE // 2, LINE // 2, LINE // 2 - 1)
    late = jnp.where(zl < LINE // 2, LINE - 1, 0)

    def wide_of(layer, first, second):
        px = (x + (1 - core) * first + core * second) % RING
        py = (y + core * first + (1 - core) * second) % RING
        return (px * 2 + (zh + layer) % 2) * RING + py

    other = (wide, zl * CORES + 1 - core)
    above, below = (wide, narrow + CORES), (wide, narrow - CORES)

    take_b = pltpu.make_async_copy(b_ref, b_all.at[pl.ds(wide * depth, depth)], local.at[0])
    take_a = pltpu.make_async_copy(a_ref, a_in, local.at[1])
    take_mask = pltpu.make_async_copy(mask_hbm, mask_ref, local.at[2])
    take_a.start()
    take_mask.start()
    take_b.start()

    barrier = pltpu.get_barrier_semaphore()

    def greet(device):
        pl.semaphore_signal(barrier, inc=1, device_id=device, device_id_type=MESH)

    for first, second in ((1, 0), (3, 0), (0, 1), (0, 3)):
        greet((wide_of(0, first, second), narrow))
    greet(other)
    peer = (wide_of(1, 0, 0), narrow)

    @pl.when(zh == 0)
    def _():
        greet(peer)

    @pl.when(zl < LINE - 1)
    def _():
        greet(above)

    @pl.when(zl > 0)
    def _():
        greet(below)

    inner = jnp.where((zl > 0) & (zl < LINE - 1), 1, 0)
    pl.semaphore_wait(barrier, 6 + inner + zh)


    def b_part(layer, first, second, part):
        base = wide_of(layer, first, second) * depth
        if part is None:
            return b_all.at[pl.ds(base, depth)]
        return b_all.at[pl.ds(base + part * half, half)]

    def b_copy(layer, first, second, part, to, label):
        where = b_part(layer, first, second, part)
        return pltpu.make_async_remote_copy(
            where,
            where,
            sb.at[0],
            zb.at[label[0], label[1] % RING, label[2] % RING, part or 0],
            device_id=(wide_of(*to), narrow),
            device_id_type=MESH,
        )

    def b_send(layer, first, second, part, step):
        df, ds = step
        b_copy(layer, first, second, part, (0, df, ds), (layer, first - df, second - ds)).start()

    def b_wait(layer, first, second, part):
        where = b_part(layer, first, second, part)
        pltpu.make_async_remote_copy(
            where,
            where,
            sb.at[0],
            zb.at[layer, first % RING, second % RING, part or 0],
            device_id=other,
            device_id_type=MESH,
        ).wait_recv()

    def b_both(layer, first, part):
        b_send(layer, first, 0, part, (0, 1))
        b_send(layer, first, 0, part, (0, 3))

    def b_begin(layer, part):
        b_send(layer, 0, 0, part, (1, 0))
        b_send(layer, 0, 0, part, (3, 0))
        b_both(layer, 0, part)

    def b_near(layer, part):
        ahead, behind = ((3, 1), (1, 3))[part]
        b_wait(layer, ahead, 0, part)
        b_send(layer, ahead, 0, part, (behind, 0))
        b_both(layer, ahead, part)
        b_wait(layer, behind, 0, part)
        b_both(layer, behind, part)

    def b_far(layer, part):
        b_wait(layer, 2, 0, part)
        b_both(layer, 2, part)

    def b_turn(layer, first):
        b_wait(layer, first, 3, 0)
        b_send(layer, first, 3, 0, (0, 1))
        b_wait(layer, first, 1, 1)
        b_send(layer, first, 1, 1, (0, 3))

    def b_end(layer):
        for first in range(RING):
            b_wait(layer, first, 3, 1)
            b_wait(layer, first, 1, 0)
            b_wait(layer, first, 2, 0)
            b_wait(layer, first, 2, 1)

    swaps = [b_copy(0, 0, 0, part, (1, 0, 0), (1, 0, 0)) for part in (0, 1)]
    take_b.wait()

    @pl.when(zh == 1)
    def _():
        pl.semaphore_signal(ready, inc=1, device_id=peer, device_id_type=MESH)
        for swap in swaps:
            swap.start()

    def a_copy(source, r, send, recv, device):
        where = a_all.at[source, core, pl.ds(pl.multiple_of(r * CHUNK, CHUNK), CHUNK)]
        return pltpu.make_async_remote_copy(
            where, where, send.at[source], recv, device_id=device, device_id_type=MESH
        )

    def over(source, r):
        return a_copy(source, r, side, ca.at[source, jnp.where(source == late, r, 0)], other)

    def upward(source, r):
        return a_copy(source, r, up, za.at[source, r], above)

    def downward(source, r):
        return a_copy(source, r, down, za.at[source, r], below)

    def from_other(where, r, source):
        pltpu.make_async_remote_copy(
            where, where, side.at[source], ca.at[source, r], device_id=other, device_id_type=MESH
        ).wait_recv()

    take_a.wait()
    take_mask.wait()

    def own(r, _):
        span = pl.ds(pl.multiple_of(r * CHUNK, CHUNK), CHUNK)
        keep = mask_ref[0, r * CHUNK // VB].astype(jnp.float32)
        a_all[zl, core, span, :] = (a_in[span, :].astype(jnp.float32) * keep).astype(jnp.bfloat16)

        @pl.when(zl < LINE - 1)
        def _():
            upward(zl, r).start()

        @pl.when(zl > 0)
        def _():
            downward(zl, r).start()

        over(zl, r).start()
        return 0

    b_begin(0, 0)
    b_begin(0, 1)
    held_back = jnp.where((inner == 0) & (zh == 0), AHEAD, chunks)
    lax.fori_loop(0, held_back, own, 0)

    def forward(distance, r):
        @pl.when(zl - distance >= 0)
        def _():
            upward(zl - distance, r).wait_recv()

            @pl.when(zl < LINE - 1)
            def _():
                upward(zl - distance, r).start()

            over(zl - distance, r).start()

        @pl.when(zl + distance < LINE)
        def _():
            downward(zl + distance, r).wait_recv()

            @pl.when(zl > 0)
            def _():
                downward(zl + distance, r).start()

            over(zl + distance, r).start()

    def forwards(distance, start, stop):
        def body(r, _):
            forward(distance, r)
            return 0

        lax.fori_loop(start * chunks // 16, stop * chunks // 16, body, 0)

    def tile(place, c, span):
        return a_all[place, c, span, :]

    def deep(place, c):
        return pl.ds(pl.multiple_of((place * CORES + c) * width, width), width)

    def multiply(places, span, start):
        left = jnp.concatenate([tile(place, c, span) for place, c in places], axis=1)
        right = jnp.concatenate([b_all[deep(place, c), start : start + COLS] for place, c in places], axis=0)
        return jnp.dot(left, right, preferred_element_type=jnp.float32)

    columns = out_ref.shape[1]
    talls = total.shape[0] // TALL
    rest_talls = REST // TALL

    def first_part(q, into, skip):
        span = pl.ds(pl.multiple_of((q + skip) * TALL, TALL), TALL)
        here = pl.ds(pl.multiple_of(q * TALL, TALL), TALL)
        for start in range(0, columns, COLS):
            into[here, start : start + COLS] = multiply([(near, zh), (near + 1, zh)], span, start)

    def second_part(q, into, skip):
        span = pl.ds(pl.multiple_of((q + skip) * TALL, TALL), TALL)
        here = pl.ds(pl.multiple_of(q * TALL, TALL), TALL)
        places = [(near, 1 - zh), (near + 1, 1 - zh), (middle, 0), (middle, 1)]
        for start in range(0, columns, COLS):
            into[here, start : start + COLS] += multiply(places, span, start)

    def parts(part, distance, first_chunk, last_chunk):
        per = (last_chunk - first_chunk) // (talls + rest_talls)

        def body(q, _):
            part(q, total, 0)
            for i in range(per):
                forward(distance, first_chunk + q * per + i)
            return 0

        def rest_body(q, _):
            part(q, total_rest, talls)
            for i in range(per):
                forward(distance, first_chunk + (talls + q) * per + i)
            return 0

        lax.fori_loop(0, talls, body, 0)
        lax.fori_loop(0, rest_talls, rest_body, 0)

    def slice_of(q):
        if q < talls:
            first_part(q, total, 0)
        else:
            first_part(q - talls, total_rest, talls)

    b_near(0, 0)
    b_near(0, 1)
    b_turn(0, 0)

    @pl.when(zh == 0)
    def _():
        pl.semaphore_wait(ready, 1)
        for swap in swaps:
            swap.start()

    lax.fori_loop(held_back, chunks, own, 0)
    b_far(0, 0)
    b_far(0, 1)
    b_turn(0, 3)
    forwards(1, 0, 6)
    b_turn(0, 1)
    forwards(1, 6, 10)
    b_turn(0, 2)
    forwards(1, 10, 12)
    b_wait(1, 0, 0, 0)
    b_begin(1, 0)
    forwards(1, 12, 14)
    b_wait(1, 0, 0, 1)
    b_begin(1, 1)
    b_near(1, 0)
    forwards(1, 14, 16)
    b_near(1, 1)
    b_end(0)
    for i in range(2):
        from_other(a_all.at[near + i, 1 - core], 0, near + i)
    b_far(1, 0)
    slice_of(0)
    b_turn(1, 0)
    b_far(1, 1)
    slice_of(1)
    forwards(2, 0, 2)
    b_turn(1, 3)
    slice_of(2)
    forwards(2, 2, 5)
    b_turn(1, 1)
    slice_of(3)
    forwards(2, 5, 8)
    b_turn(1, 2)
    forwards(2, 8, 16)
    b_end(1)
    from_other(a_all.at[middle, 1 - core], 0, middle)
    b_rest[...] = b_all[pl.ds(pl.multiple_of(late * CORES * width, CORES * width), CORES * width)]
    parts(second_part, 3, 0, 8)

    def arrive(start, stop):
        def body(r, _):
            from_other(a_all.at[late, 1 - core, pl.ds(pl.multiple_of(r * CHUNK, CHUNK), CHUNK)], r, late)
            return 0

        lax.fori_loop(start, stop, body, 0)

    def final(q):
        span = pl.ds(pl.multiple_of(q * BLOCK, BLOCK), BLOCK)
        for start in range(0, columns, COLS):
            out_ref[span, start : start + COLS] = (
                total[span, start : start + COLS] + multiply([(late, 0), (late, 1)], span, start)
            ).astype(out_ref.dtype)

    blocks = total.shape[0] // BLOCK
    per = BLOCK // CHUNK

    def last_part(q, _):
        forward(3, chunks // 2 + q)
        arrive(q * per, (q + 1) * per)
        final(q)
        return 0

    lax.fori_loop(0, blocks, last_part, 0)

    def last_forward(r, _):
        forward(3, r)
        return 0

    lax.fori_loop(chunks // 2 + blocks, chunks, last_forward, 0)
    arrive(blocks * per, chunks)
    for c in range(CORES):
        a_rest[:, c * width : (c + 1) * width] = a_all[late, c, pl.ds(rows - REST, REST), :]

    everything = b_all.at[pl.ds(0, b_all.shape[0] - depth)]
    pltpu.make_async_remote_copy(
        everything, everything, sb.at[0], zb.at[0, 0, 0, 0], device_id=other, device_id_type=MESH
    ).wait_send()

    def finish(source, _):
        def sent(sem):
            where = a_all.at[source, core]
            pltpu.make_async_remote_copy(
                where, where, sem.at[source], za.at[0, 0], device_id=other, device_id_type=MESH
            ).wait_send()

        sent(side)

        @pl.when((source <= zl) & (zl < LINE - 1))
        def _():
            sent(up)

        @pl.when((source >= zl) & (zl > 0))
        def _():
            sent(down)

        return 0

    lax.fori_loop(0, LINE, finish, 0)


def finish_rows(done_ref, total_ref, a_ref, b_ref, to_ref, last, sem):
    size, done = BLOCK, done_ref.shape[0]
    copies = []

    def send(where, row):
        copy = pltpu.make_async_copy(where, to_ref.at[pl.ds(row, size)], sem.at[len(copies)])
        copy.start()
        copies.append(copy)

    for row in range(0, done, size):
        send(done_ref.at[pl.ds(row, size)], row)
    for row in range(0, last.shape[0], size):
        for start in range(0, last.shape[1], COLS):
            last[row : row + size, start : start + COLS] = (
                total_ref[row : row + size, start : start + COLS]
                + jnp.dot(
                    a_ref[row : row + size], b_ref[:, start : start + COLS], preferred_element_type=jnp.float32
                )
            ).astype(last.dtype)
        send(last.at[pl.ds(row, size)], done + row)
    for copy in copies:
        copy.wait()


def shards(amplitudes, pair_mask, integrals):
    rows, width = amplitudes.shape
    depth, columns = integrals.shape
    deep = depth * 2 * RING * RING
    chunks = rows // CHUNK
    dma = pltpu.SemaphoreType.DMA
    held = pl.pallas_call(
        kernel,
        out_shape=[
            jax.ShapeDtypeStruct((rows - REST, columns), jnp.bfloat16),
            jax.ShapeDtypeStruct((REST, columns), jnp.float32),
            jax.ShapeDtypeStruct((REST, CORES * width), jnp.bfloat16),
            jax.ShapeDtypeStruct((CORES * width, columns), jnp.bfloat16),
        ],
        in_specs=[
            pl.BlockSpec(memory_space=pltpu.HBM),
            pl.BlockSpec(memory_space=pltpu.HBM),
            pl.BlockSpec(memory_space=pltpu.HBM),
        ],
        out_specs=[pl.BlockSpec(memory_space=pltpu.VMEM)] * 4,
        scratch_shapes=[
            pltpu.SMEM((1, rows // VB), jnp.int32),
            pltpu.VMEM((rows, width), jnp.bfloat16),
            pltpu.VMEM((LINE, CORES, rows, width), jnp.bfloat16),
            pltpu.VMEM((deep, columns), jnp.bfloat16),
            pltpu.VMEM((rows - REST, columns), jnp.float32),
            dma((3,)),
            dma((LINE, chunks)),
            dma((LINE, chunks)),
            dma((LINE,)),
            dma((LINE,)),
            dma((LINE,)),
            dma((2, RING, RING, 2)),
            dma((1,)),
            pltpu.SemaphoreType.REGULAR,
        ],
        compiler_params=pltpu.CompilerParams(
            collective_id=0, has_side_effects=True, vmem_limit_bytes=40 * 2**20
        ),
        cost_estimate=pl.CostEstimate(
            flops=2 * rows * columns * deep, bytes_accessed=2 * rows * columns, transcendentals=0
        ),
    )(*[pltpu.with_memory_space_constraint(v, pltpu.HBM) for v in (pair_mask.reshape(1, -1), amplitudes, integrals)])
    return pl.pallas_call(
        finish_rows,
        out_shape=jax.ShapeDtypeStruct((rows, columns), jnp.bfloat16),
        in_specs=[pl.BlockSpec(memory_space=pltpu.VMEM)] * 4,
        out_specs=pl.BlockSpec(memory_space=pltpu.HBM),
        scratch_shapes=[pltpu.VMEM((REST, columns), jnp.bfloat16), dma((rows // BLOCK,))],
        compiler_params=pltpu.CompilerParams(vmem_limit_bytes=20 * 2**20),
        cost_estimate=pl.CostEstimate(
            flops=2 * REST * columns * CORES * width, bytes_accessed=2 * rows * columns, transcendentals=0
        ),
    )(*held)


def solution(mesh):
    placed = P("wide", "narrow")
    return jax.shard_map(
        shards, mesh=mesh, in_specs=(placed, placed, placed), out_specs=placed, check_vma=False
    )
```

```python
import functools

import jax
import jax.numpy as jnp
from jax import lax
from jax.experimental import pallas as pl
from jax.experimental.pallas import tpu as pltpu
from jax.sharding import PartitionSpec as P

MESH = pl.DeviceIdType.MESH
VB = 128
LINE = 4
RING = 4
CORES = 2
CHUNK = 128
BLOCK = 256
TALL = 512
REST = 1024
AHEAD = 6
COLS = 512


def kernel(
    mask_hbm,
    a_ref,
    b_ref,
    out_ref,
    total_rest,
    a_rest,
    b_rest,
    mask_ref,
    a_in,
    a_all,
    b_all,
    total,
    local,
    za,
    ca,
    up,
    down,
    side,
    zb,
    sb,
    ready,
):
    wide, narrow = lax.axis_index("wide"), lax.axis_index("narrow")
    zl, core = narrow // CORES, narrow % CORES
    x, zh, y = wide // (2 * RING), (wide // RING) % 2, wide % RING
    rows, width = a_in.shape
    depth = b_ref.shape[0]
    half = depth // 2
    chunks = rows // CHUNK
    near = jnp.where(zl < LINE // 2, 0, LINE // 2)
    middle = jnp.where(zl < LINE // 2, LINE // 2, LINE // 2 - 1)
    late = jnp.where(zl < LINE // 2, LINE - 1, 0)

    def wide_of(layer, first, second):
        px = (x + (1 - core) * first + core * second) % RING
        py = (y + core * first + (1 - core) * second) % RING
        return (px * 2 + (zh + layer) % 2) * RING + py

    other = (wide, zl * CORES + 1 - core)
    above, below = (wide, narrow + CORES), (wide, narrow - CORES)

    take_b = pltpu.make_async_copy(b_ref, b_all.at[pl.ds(wide * depth, depth)], local.at[0])
    take_a = pltpu.make_async_copy(a_ref, a_in, local.at[1])
    take_mask = pltpu.make_async_copy(mask_hbm, mask_ref, local.at[2])
    take_a.start()
    take_mask.start()
    take_b.start()

    barrier = pltpu.get_barrier_semaphore()

    def greet(device):
        pl.semaphore_signal(barrier, inc=1, device_id=device, device_id_type=MESH)

    peer = (wide_of(1, 0, 0), narrow)

    def to_x(px):
        return (((px + RING) % RING * 2 + zh) * RING + y, narrow)

    def to_y(py):
        return ((x * 2 + zh) * RING + (py + RING) % RING, narrow)

    higher = (
        (x < RING - 1, to_x(x + 1), 1),
        (x == 0, to_x(RING - 1), 1),
        (y < RING - 1, to_y(y + 1), 1),
        (y == 0, to_y(RING - 1), 1),
        (zl < LINE - 1, above, 0),
        (zh == 0, peer, 2),
    )
    lower = (
        (x > 0, to_x(x - 1), 1),
        (x == RING - 1, to_x(0), 1),
        (y > 0, to_y(y - 1), 1),
        (y == RING - 1, to_y(0), 1),
        (zl > 0, below, 0),
        (zh == 1, peer, 2),
    )
    greet(other)
    for present, device, _ in higher:
        pl.when(present)(functools.partial(greet, device))

    def count(*conditions):
        return sum(jnp.where(c, 1, 0) for c in conditions)

    before = count(*(present for present, _, _ in lower))
    pl.semaphore_wait(barrier, 1 + before)
    for present, device, kind in lower:
        pl.when(present)(
            functools.partial(
                pl.semaphore_signal, ready.at[kind], inc=1, device_id=device, device_id_type=MESH
            )
        )
    inner = jnp.where((zl > 0) & (zl < LINE - 1), 1, 0)
    in_plane = count(*(present for present, _, kind in higher if kind == 1))


    def b_part(layer, first, second, part):
        base = wide_of(layer, first, second) * depth
        if part is None:
            return b_all.at[pl.ds(base, depth)]
        return b_all.at[pl.ds(base + part * half, half)]

    def b_copy(layer, first, second, part, to, label):
        where = b_part(layer, first, second, part)
        return pltpu.make_async_remote_copy(
            where,
            where,
            sb.at[0],
            zb.at[label[0], label[1] % RING, label[2] % RING, part or 0],
            device_id=(wide_of(*to), narrow),
            device_id_type=MESH,
        )

    def b_send(layer, first, second, part, step):
        df, ds = step
        b_copy(layer, first, second, part, (0, df, ds), (layer, first - df, second - ds)).start()

    def b_wait(layer, first, second, part):
        where = b_part(layer, first, second, part)
        pltpu.make_async_remote_copy(
            where,
            where,
            sb.at[0],
            zb.at[layer, first % RING, second % RING, part or 0],
            device_id=other,
            device_id_type=MESH,
        ).wait_recv()

    def b_both(layer, first, part):
        b_send(layer, first, 0, part, (0, 1))
        b_send(layer, first, 0, part, (0, 3))

    def b_begin(layer, part):
        b_send(layer, 0, 0, part, (1, 0))
        b_send(layer, 0, 0, part, (3, 0))
        b_both(layer, 0, part)

    def b_near(layer, part):
        ahead, behind = ((3, 1), (1, 3))[part]
        b_wait(layer, ahead, 0, part)
        b_send(layer, ahead, 0, part, (behind, 0))
        b_both(layer, ahead, part)
        b_wait(layer, behind, 0, part)
        b_both(layer, behind, part)

    def b_far(layer, part):
        b_wait(layer, 2, 0, part)
        b_both(layer, 2, part)

    def b_turn(layer, first):
        b_wait(layer, first, 3, 0)
        b_send(layer, first, 3, 0, (0, 1))
        b_wait(layer, first, 1, 1)
        b_send(layer, first, 1, 1, (0, 3))

    def b_end(layer):
        for first in range(RING):
            b_wait(layer, first, 3, 1)
            b_wait(layer, first, 1, 0)
            b_wait(layer, first, 2, 0)
            b_wait(layer, first, 2, 1)

    swaps = [b_copy(0, 0, 0, part, (1, 0, 0), (1, 0, 0)) for part in (0, 1)]
    take_b.wait()

    @pl.when(zh == 1)
    def _():
        for swap in swaps:
            swap.start()

    def a_copy(source, r, send, recv, device):
        where = a_all.at[source, core, pl.ds(pl.multiple_of(r * CHUNK, CHUNK), CHUNK)]
        return pltpu.make_async_remote_copy(
            where, where, send.at[source], recv, device_id=device, device_id_type=MESH
        )

    def over(source, r):
        return a_copy(source, r, side, ca.at[source, jnp.where(source == late, r, 0)], other)

    def upward(source, r):
        return a_copy(source, r, up, za.at[source, r], above)

    def downward(source, r):
        return a_copy(source, r, down, za.at[source, r], below)

    def from_other(where, r, source):
        pltpu.make_async_remote_copy(
            where, where, side.at[source], ca.at[source, r], device_id=other, device_id_type=MESH
        ).wait_recv()

    take_a.wait()
    take_mask.wait()

    def own(r, _):
        span = pl.ds(pl.multiple_of(r * CHUNK, CHUNK), CHUNK)
        keep = mask_ref[0, r * CHUNK // VB].astype(jnp.float32)
        a_all[zl, core, span, :] = (a_in[span, :].astype(jnp.float32) * keep).astype(jnp.bfloat16)

        @pl.when(zl > 0)
        def _():
            downward(zl, r).start()

        over(zl, r).start()
        return 0

    def own_up(r, _):
        upward(zl, r).start()
        return 0

    def own_ups(start, stop):
        @pl.when(zl < LINE - 1)
        def _():
            lax.fori_loop(start, stop, own_up, 0)

    held_back = jnp.where((inner == 0) & (zh == 0), AHEAD, chunks)
    lax.fori_loop(0, held_back, own, 0)

    @pl.when(zl < LINE - 1)
    def _():
        pl.semaphore_wait(ready.at[0], 1)

    own_ups(0, held_back)

    @pl.when(in_plane > 0)
    def _():
        pl.semaphore_wait(ready.at[1], in_plane)

    b_begin(0, 0)
    b_begin(0, 1)

    def forward(distance, r):
        @pl.when(zl - distance >= 0)
        def _():
            upward(zl - distance, r).wait_recv()

            @pl.when(zl < LINE - 1)
            def _():
                upward(zl - distance, r).start()

            over(zl - distance, r).start()

        @pl.when(zl + distance < LINE)
        def _():
            downward(zl + distance, r).wait_recv()

            @pl.when(zl > 0)
            def _():
                downward(zl + distance, r).start()

            over(zl + distance, r).start()

    def forwards(distance, start, stop):
        def body(r, _):
            forward(distance, r)
            return 0

        lax.fori_loop(start * chunks // 16, stop * chunks // 16, body, 0)

    def tile(place, c, span):
        return a_all[place, c, span, :]

    def deep(place, c):
        return pl.ds(pl.multiple_of((place * CORES + c) * width, width), width)

    def multiply(places, span, start):
        left = jnp.concatenate([tile(place, c, span) for place, c in places], axis=1)
        right = jnp.concatenate([b_all[deep(place, c), start : start + COLS] for place, c in places], axis=0)
        return jnp.dot(left, right, preferred_element_type=jnp.float32)

    columns = out_ref.shape[1]
    talls = total.shape[0] // TALL
    rest_talls = REST // TALL

    def first_part(q, into, skip):
        span = pl.ds(pl.multiple_of((q + skip) * TALL, TALL), TALL)
        here = pl.ds(pl.multiple_of(q * TALL, TALL), TALL)
        for start in range(0, columns, COLS):
            into[here, start : start + COLS] = multiply([(near, zh), (near + 1, zh)], span, start)

    def second_part(q, into, skip):
        span = pl.ds(pl.multiple_of((q + skip) * TALL, TALL), TALL)
        here = pl.ds(pl.multiple_of(q * TALL, TALL), TALL)
        places = [(near, 1 - zh), (near + 1, 1 - zh), (middle, 0), (middle, 1)]
        for start in range(0, columns, COLS):
            into[here, start : start + COLS] += multiply(places, span, start)

    def parts(part, distance, first_chunk, last_chunk):
        per = (last_chunk - first_chunk) // (talls + rest_talls)

        def body(q, _):
            part(q, total, 0)
            for i in range(per):
                forward(distance, first_chunk + q * per + i)
            return 0

        def rest_body(q, _):
            part(q, total_rest, talls)
            for i in range(per):
                forward(distance, first_chunk + (talls + q) * per + i)
            return 0

        lax.fori_loop(0, talls, body, 0)
        lax.fori_loop(0, rest_talls, rest_body, 0)

    def slice_of(q):
        if q < talls:
            first_part(q, total, 0)
        else:
            first_part(q - talls, total_rest, talls)

    b_near(0, 0)
    b_near(0, 1)
    b_turn(0, 0)

    @pl.when(zh == 0)
    def _():
        pl.semaphore_wait(ready.at[2], 1)
        for swap in swaps:
            swap.start()

    lax.fori_loop(held_back, chunks, own, 0)
    own_ups(held_back, chunks)
    b_far(0, 0)
    b_far(0, 1)
    b_turn(0, 3)
    forwards(1, 0, 6)
    b_turn(0, 1)
    forwards(1, 6, 10)
    b_turn(0, 2)
    forwards(1, 10, 12)
    b_wait(1, 0, 0, 0)
    b_begin(1, 0)
    forwards(1, 12, 14)
    b_wait(1, 0, 0, 1)
    b_begin(1, 1)
    b_near(1, 0)
    forwards(1, 14, 16)
    b_near(1, 1)
    b_end(0)
    for i in range(2):
        from_other(a_all.at[near + i, 1 - core], 0, near + i)
    b_far(1, 0)
    slice_of(0)
    b_turn(1, 0)
    b_far(1, 1)
    slice_of(1)
    forwards(2, 0, 2)
    b_turn(1, 3)
    slice_of(2)
    forwards(2, 2, 5)
    b_turn(1, 1)
    slice_of(3)
    forwards(2, 5, 8)
    b_turn(1, 2)
    forwards(2, 8, 16)
    b_end(1)
    from_other(a_all.at[middle, 1 - core], 0, middle)
    b_rest[...] = b_all[pl.ds(pl.multiple_of(late * CORES * width, CORES * width), CORES * width)]
    parts(second_part, 3, 0, 8)

    def arrive(start, stop):
        def body(r, _):
            from_other(a_all.at[late, 1 - core, pl.ds(pl.multiple_of(r * CHUNK, CHUNK), CHUNK)], r, late)
            return 0

        lax.fori_loop(start, stop, body, 0)

    def final(q):
        span = pl.ds(pl.multiple_of(q * BLOCK, BLOCK), BLOCK)
        for start in range(0, columns, COLS):
            out_ref[span, start : start + COLS] = (
                total[span, start : start + COLS] + multiply([(late, 0), (late, 1)], span, start)
            ).astype(out_ref.dtype)

    blocks = total.shape[0] // BLOCK
    per = BLOCK // CHUNK

    def last_part(q, _):
        forward(3, chunks // 2 + q)
        arrive(q * per, (q + 1) * per)
        final(q)
        return 0

    lax.fori_loop(0, blocks, last_part, 0)

    def last_forward(r, _):
        forward(3, r)
        return 0

    lax.fori_loop(chunks // 2 + blocks, chunks, last_forward, 0)
    arrive(blocks * per, chunks)
    for c in range(CORES):
        a_rest[:, c * width : (c + 1) * width] = a_all[late, c, pl.ds(rows - REST, REST), :]

    everything = b_all.at[pl.ds(0, b_all.shape[0] - depth)]
    pltpu.make_async_remote_copy(
        everything, everything, sb.at[0], zb.at[0, 0, 0, 0], device_id=other, device_id_type=MESH
    ).wait_send()

    def finish(source, _):
        def sent(sem):
            where = a_all.at[source, core]
            pltpu.make_async_remote_copy(
                where, where, sem.at[source], za.at[0, 0], device_id=other, device_id_type=MESH
            ).wait_send()

        sent(side)

        @pl.when((source <= zl) & (zl < LINE - 1))
        def _():
            sent(up)

        @pl.when((source >= zl) & (zl > 0))
        def _():
            sent(down)

        return 0

    lax.fori_loop(0, LINE, finish, 0)


def finish_rows(done_ref, total_ref, a_ref, b_ref, to_ref, last, sem):
    size, done = BLOCK, done_ref.shape[0]
    copies = []

    def send(where, row):
        copy = pltpu.make_async_copy(where, to_ref.at[pl.ds(row, size)], sem.at[len(copies)])
        copy.start()
        copies.append(copy)

    for row in range(0, done, size):
        send(done_ref.at[pl.ds(row, size)], row)
    for row in range(0, last.shape[0], size):
        for start in range(0, last.shape[1], COLS):
            last[row : row + size, start : start + COLS] = (
                total_ref[row : row + size, start : start + COLS]
                + jnp.dot(
                    a_ref[row : row + size], b_ref[:, start : start + COLS], preferred_element_type=jnp.float32
                )
            ).astype(last.dtype)
        send(last.at[pl.ds(row, size)], done + row)
    for copy in copies:
        copy.wait()


def shards(amplitudes, pair_mask, integrals):
    rows, width = amplitudes.shape
    depth, columns = integrals.shape
    deep = depth * 2 * RING * RING
    chunks = rows // CHUNK
    dma = pltpu.SemaphoreType.DMA
    held = pl.pallas_call(
        kernel,
        out_shape=[
            jax.ShapeDtypeStruct((rows - REST, columns), jnp.bfloat16),
            jax.ShapeDtypeStruct((REST, columns), jnp.float32),
            jax.ShapeDtypeStruct((REST, CORES * width), jnp.bfloat16),
            jax.ShapeDtypeStruct((CORES * width, columns), jnp.bfloat16),
        ],
        in_specs=[
            pl.BlockSpec(memory_space=pltpu.HBM),
            pl.BlockSpec(memory_space=pltpu.HBM),
            pl.BlockSpec(memory_space=pltpu.HBM),
        ],
        out_specs=[pl.BlockSpec(memory_space=pltpu.VMEM)] * 4,
        scratch_shapes=[
            pltpu.SMEM((1, rows // VB), jnp.int32),
            pltpu.VMEM((rows, width), jnp.bfloat16),
            pltpu.VMEM((LINE, CORES, rows, width), jnp.bfloat16),
            pltpu.VMEM((deep, columns), jnp.bfloat16),
            pltpu.VMEM((rows - REST, columns), jnp.float32),
            dma((3,)),
            dma((LINE, chunks)),
            dma((LINE, chunks)),
            dma((LINE,)),
            dma((LINE,)),
            dma((LINE,)),
            dma((2, RING, RING, 2)),
            dma((1,)),
            pltpu.SemaphoreType.REGULAR((3,)),
        ],
        compiler_params=pltpu.CompilerParams(
            collective_id=0, has_side_effects=True, vmem_limit_bytes=40 * 2**20
        ),
        cost_estimate=pl.CostEstimate(
            flops=2 * rows * columns * deep, bytes_accessed=2 * rows * columns, transcendentals=0
        ),
    )(*[pltpu.with_memory_space_constraint(v, pltpu.HBM) for v in (pair_mask.reshape(1, -1), amplitudes, integrals)])
    return pl.pallas_call(
        finish_rows,
        out_shape=jax.ShapeDtypeStruct((rows, columns), jnp.bfloat16),
        in_specs=[pl.BlockSpec(memory_space=pltpu.VMEM)] * 4,
        out_specs=pl.BlockSpec(memory_space=pltpu.HBM),
        scratch_shapes=[pltpu.VMEM((REST, columns), jnp.bfloat16), dma((rows // BLOCK,))],
        compiler_params=pltpu.CompilerParams(vmem_limit_bytes=20 * 2**20),
        cost_estimate=pl.CostEstimate(
            flops=2 * REST * columns * CORES * width, bytes_accessed=2 * rows * columns, transcendentals=0
        ),
    )(*held)


def solution(mesh):
    placed = P("wide", "narrow")
    return jax.shard_map(
        shards, mesh=mesh, in_specs=(placed, placed, placed), out_specs=placed, check_vma=False
    )
```

```python
import functools

import jax
import jax.numpy as jnp
from jax import lax
from jax.experimental import pallas as pl
from jax.experimental.pallas import tpu as pltpu
from jax.sharding import PartitionSpec as P

MESH = pl.DeviceIdType.MESH
VB = 128
LINE = 4
RING = 4
CORES = 2
CHUNK = 128
BLOCK = 256
TALL = 512
REST = 1024
AHEAD = 6
COLS = 512


def kernel(
    mask_hbm,
    a_ref,
    b_ref,
    out_ref,
    total_rest,
    a_rest,
    b_rest,
    mask_ref,
    a_in,
    a_all,
    b_all,
    total,
    local,
    za,
    ca,
    up,
    down,
    side,
    zb,
    sb,
    ready,
):
    wide, narrow = lax.axis_index("wide"), lax.axis_index("narrow")
    zl, core = narrow // CORES, narrow % CORES
    x, zh, y = wide // (2 * RING), (wide // RING) % 2, wide % RING
    rows, width = a_in.shape
    depth = b_ref.shape[0]
    half = depth // 2
    chunks = rows // CHUNK
    near = jnp.where(zl < LINE // 2, 0, LINE // 2)
    middle = jnp.where(zl < LINE // 2, LINE // 2, LINE // 2 - 1)
    late = jnp.where(zl < LINE // 2, LINE - 1, 0)

    def wide_of(layer, first, second):
        px = (x + (1 - core) * first + core * second) % RING
        py = (y + core * first + (1 - core) * second) % RING
        return (px * 2 + (zh + layer) % 2) * RING + py

    other = (wide, zl * CORES + 1 - core)
    above, below = (wide, narrow + CORES), (wide, narrow - CORES)

    take_b = pltpu.make_async_copy(b_ref, b_all.at[pl.ds(wide * depth, depth)], local.at[0])
    take_a = pltpu.make_async_copy(a_ref, a_in, local.at[1])
    take_mask = pltpu.make_async_copy(mask_hbm, mask_ref, local.at[2])
    take_a.start()
    take_mask.start()
    take_b.start()

    barrier = pltpu.get_barrier_semaphore()

    def greet(device):
        pl.semaphore_signal(barrier, inc=1, device_id=device, device_id_type=MESH)

    peer = (wide_of(1, 0, 0), narrow)

    def to_x(px):
        return (((px + RING) % RING * 2 + zh) * RING + y, narrow)

    def to_y(py):
        return ((x * 2 + zh) * RING + (py + RING) % RING, narrow)

    higher = (
        (x < RING - 1, to_x(x + 1), 1),
        (x == 0, to_x(RING - 1), 1),
        (y < RING - 1, to_y(y + 1), 1),
        (y == 0, to_y(RING - 1), 1),
        (zl < LINE - 1, above, 0),
        (zh == 0, peer, 2),
    )
    lower = (
        (x > 0, to_x(x - 1), 1),
        (x == RING - 1, to_x(0), 1),
        (y > 0, to_y(y - 1), 1),
        (y == RING - 1, to_y(0), 1),
        (zl > 0, below, 0),
        (zh == 1, peer, 2),
    )
    greet(other)
    for present, device, _ in higher:
        pl.when(present)(functools.partial(greet, device))

    def count(*conditions):
        return sum(jnp.where(c, 1, 0) for c in conditions)

    before = count(*(present for present, _, _ in lower))
    pl.semaphore_wait(barrier, 1 + before)
    for present, device, kind in lower:
        pl.when(present)(
            functools.partial(
                pl.semaphore_signal, ready.at[kind], inc=1, device_id=device, device_id_type=MESH
            )
        )
    inner = jnp.where((zl > 0) & (zl < LINE - 1), 1, 0)
    in_plane = count(*(present for present, _, kind in higher if kind == 1))


    def b_part(layer, first, second, part):
        base = wide_of(layer, first, second) * depth
        if part is None:
            return b_all.at[pl.ds(base, depth)]
        return b_all.at[pl.ds(base + part * half, half)]

    def b_copy(layer, first, second, part, to, label):
        where = b_part(layer, first, second, part)
        return pltpu.make_async_remote_copy(
            where,
            where,
            sb.at[0],
            zb.at[label[0], label[1] % RING, label[2] % RING, part or 0],
            device_id=(wide_of(*to), narrow),
            device_id_type=MESH,
        )

    def b_send(layer, first, second, part, step):
        df, ds = step
        b_copy(layer, first, second, part, (0, df, ds), (layer, first - df, second - ds)).start()

    def b_wait(layer, first, second, part):
        where = b_part(layer, first, second, part)
        pltpu.make_async_remote_copy(
            where,
            where,
            sb.at[0],
            zb.at[layer, first % RING, second % RING, part or 0],
            device_id=other,
            device_id_type=MESH,
        ).wait_recv()

    def b_both(layer, first, part):
        b_send(layer, first, 0, part, (0, 1))
        b_send(layer, first, 0, part, (0, 3))

    def b_begin(layer, part):
        b_send(layer, 0, 0, part, (1, 0))
        b_send(layer, 0, 0, part, (3, 0))
        b_both(layer, 0, part)

    def b_near(layer, part):
        ahead, behind = ((3, 1), (1, 3))[part]
        b_wait(layer, ahead, 0, part)
        b_send(layer, ahead, 0, part, (behind, 0))
        b_both(layer, ahead, part)
        b_wait(layer, behind, 0, part)
        b_both(layer, behind, part)

    def b_far(layer, part):
        b_wait(layer, 2, 0, part)
        b_both(layer, 2, part)

    def b_turn(layer, first):
        b_wait(layer, first, 3, 0)
        b_send(layer, first, 3, 0, (0, 1))
        b_wait(layer, first, 1, 1)
        b_send(layer, first, 1, 1, (0, 3))

    def b_end(layer):
        for first in range(RING):
            b_wait(layer, first, 3, 1)
            b_wait(layer, first, 1, 0)
            b_wait(layer, first, 2, 0)
            b_wait(layer, first, 2, 1)

    swaps = [b_copy(0, 0, 0, part, (1, 0, 0), (1, 0, 0)) for part in (0, 1)]
    take_b.wait()

    @pl.when(zh == 1)
    def _():
        for swap in swaps:
            swap.start()

    def a_copy(source, r, send, recv, device):
        where = a_all.at[source, core, pl.ds(pl.multiple_of(r * CHUNK, CHUNK), CHUNK)]
        return pltpu.make_async_remote_copy(
            where, where, send.at[source], recv, device_id=device, device_id_type=MESH
        )

    def over(source, r):
        return a_copy(source, r, side, ca.at[source, jnp.where(source == late, r, 0)], other)

    def upward(source, r):
        return a_copy(source, r, up, za.at[source, r], above)

    def downward(source, r):
        return a_copy(source, r, down, za.at[source, r], below)

    def from_other(where, r, source):
        pltpu.make_async_remote_copy(
            where, where, side.at[source], ca.at[source, r], device_id=other, device_id_type=MESH
        ).wait_recv()

    take_a.wait()
    take_mask.wait()

    def own(r, _):
        span = pl.ds(pl.multiple_of(r * CHUNK, CHUNK), CHUNK)
        keep = mask_ref[0, r * CHUNK // VB].astype(jnp.float32)
        a_all[zl, core, span, :] = (a_in[span, :].astype(jnp.float32) * keep).astype(jnp.bfloat16)

        @pl.when(zl > 0)
        def _():
            downward(zl, r).start()

        over(zl, r).start()
        return 0

    def own_up(r, _):
        upward(zl, r).start()
        return 0

    def own_ups(start, stop):
        @pl.when(zl < LINE - 1)
        def _():
            lax.fori_loop(start, stop, own_up, 0)

    ahead = jnp.where(inner == 0, AHEAD, jnp.where(zl == LINE // 2, 2 * AHEAD, chunks))
    held_back = jnp.where(zh == 0, ahead, chunks)
    lax.fori_loop(0, held_back, own, 0)

    @pl.when(zl < LINE - 1)
    def _():
        pl.semaphore_wait(ready.at[0], 1)

    own_ups(0, held_back)

    @pl.when(in_plane > 0)
    def _():
        pl.semaphore_wait(ready.at[1], in_plane)

    b_begin(0, 0)
    b_begin(0, 1)

    def forward(distance, r):
        @pl.when(zl - distance >= 0)
        def _():
            upward(zl - distance, r).wait_recv()

            @pl.when(zl < LINE - 1)
            def _():
                upward(zl - distance, r).start()

            over(zl - distance, r).start()

        @pl.when(zl + distance < LINE)
        def _():
            downward(zl + distance, r).wait_recv()

            @pl.when(zl > 0)
            def _():
                downward(zl + distance, r).start()

            over(zl + distance, r).start()

    def forwards(distance, start, stop):
        def body(r, _):
            forward(distance, r)
            return 0

        lax.fori_loop(start * chunks // 16, stop * chunks // 16, body, 0)

    def tile(place, c, span):
        return a_all[place, c, span, :]

    def deep(place, c):
        return pl.ds(pl.multiple_of((place * CORES + c) * width, width), width)

    def multiply(places, span, start):
        left = jnp.concatenate([tile(place, c, span) for place, c in places], axis=1)
        right = jnp.concatenate([b_all[deep(place, c), start : start + COLS] for place, c in places], axis=0)
        return jnp.dot(left, right, preferred_element_type=jnp.float32)

    columns = out_ref.shape[1]
    talls = total.shape[0] // TALL
    rest_talls = REST // TALL

    def first_part(q, into, skip):
        span = pl.ds(pl.multiple_of((q + skip) * TALL, TALL), TALL)
        here = pl.ds(pl.multiple_of(q * TALL, TALL), TALL)
        for start in range(0, columns, COLS):
            into[here, start : start + COLS] = multiply([(near, zh), (near + 1, zh)], span, start)

    def second_part(q, into, skip):
        span = pl.ds(pl.multiple_of((q + skip) * TALL, TALL), TALL)
        here = pl.ds(pl.multiple_of(q * TALL, TALL), TALL)
        places = [(near, 1 - zh), (near + 1, 1 - zh), (middle, 0), (middle, 1)]
        for start in range(0, columns, COLS):
            into[here, start : start + COLS] += multiply(places, span, start)

    def parts(part, distance, first_chunk, last_chunk):
        per = (last_chunk - first_chunk) // (talls + rest_talls)

        def body(q, _):
            part(q, total, 0)
            for i in range(per):
                forward(distance, first_chunk + q * per + i)
            return 0

        def rest_body(q, _):
            part(q, total_rest, talls)
            for i in range(per):
                forward(distance, first_chunk + (talls + q) * per + i)
            return 0

        lax.fori_loop(0, talls, body, 0)
        lax.fori_loop(0, rest_talls, rest_body, 0)

    def slice_of(q):
        if q < talls:
            first_part(q, total, 0)
        else:
            first_part(q - talls, total_rest, talls)

    b_near(0, 0)
    b_near(0, 1)
    b_turn(0, 0)

    @pl.when(zh == 0)
    def _():
        pl.semaphore_wait(ready.at[2], 1)
        for swap in swaps:
            swap.start()

    lax.fori_loop(held_back, chunks, own, 0)
    own_ups(held_back, chunks)
    b_far(0, 0)
    b_far(0, 1)
    b_turn(0, 3)
    forwards(1, 0, 6)
    b_turn(0, 1)
    forwards(1, 6, 10)
    b_turn(0, 2)
    forwards(1, 10, 12)
    b_wait(1, 0, 0, 0)
    b_begin(1, 0)
    forwards(1, 12, 14)
    b_wait(1, 0, 0, 1)
    b_begin(1, 1)
    b_near(1, 0)
    forwards(1, 14, 16)
    b_near(1, 1)
    b_end(0)
    for i in range(2):
        from_other(a_all.at[near + i, 1 - core], 0, near + i)
    b_far(1, 0)
    slice_of(0)
    b_turn(1, 0)
    b_far(1, 1)
    slice_of(1)
    forwards(2, 0, 2)
    b_turn(1, 3)
    slice_of(2)
    forwards(2, 2, 5)
    b_turn(1, 1)
    slice_of(3)
    forwards(2, 5, 8)
    b_turn(1, 2)
    forwards(2, 8, 16)
    b_end(1)
    from_other(a_all.at[middle, 1 - core], 0, middle)
    b_rest[...] = b_all[pl.ds(pl.multiple_of(late * CORES * width, CORES * width), CORES * width)]
    parts(second_part, 3, 0, 8)

    def arrive(start, stop):
        def body(r, _):
            from_other(a_all.at[late, 1 - core, pl.ds(pl.multiple_of(r * CHUNK, CHUNK), CHUNK)], r, late)
            return 0

        lax.fori_loop(start, stop, body, 0)

    def final(q):
        span = pl.ds(pl.multiple_of(q * BLOCK, BLOCK), BLOCK)
        for start in range(0, columns, COLS):
            out_ref[span, start : start + COLS] = (
                total[span, start : start + COLS] + multiply([(late, 0), (late, 1)], span, start)
            ).astype(out_ref.dtype)

    blocks = total.shape[0] // BLOCK
    per = BLOCK // CHUNK

    def last_part(q, _):
        forward(3, chunks // 2 + q)
        arrive(q * per, (q + 1) * per)
        final(q)
        return 0

    lax.fori_loop(0, blocks, last_part, 0)

    def last_forward(r, _):
        forward(3, r)
        return 0

    lax.fori_loop(chunks // 2 + blocks, chunks, last_forward, 0)
    arrive(blocks * per, chunks)
    for c in range(CORES):
        a_rest[:, c * width : (c + 1) * width] = a_all[late, c, pl.ds(rows - REST, REST), :]

    everything = b_all.at[pl.ds(0, b_all.shape[0] - depth)]
    pltpu.make_async_remote_copy(
        everything, everything, sb.at[0], zb.at[0, 0, 0, 0], device_id=other, device_id_type=MESH
    ).wait_send()

    def finish(source, _):
        def sent(sem):
            where = a_all.at[source, core]
            pltpu.make_async_remote_copy(
                where, where, sem.at[source], za.at[0, 0], device_id=other, device_id_type=MESH
            ).wait_send()

        sent(side)

        @pl.when((source <= zl) & (zl < LINE - 1))
        def _():
            sent(up)

        @pl.when((source >= zl) & (zl > 0))
        def _():
            sent(down)

        return 0

    lax.fori_loop(0, LINE, finish, 0)


def finish_rows(done_ref, total_ref, a_ref, b_ref, to_ref, last, sem):
    size, done = BLOCK, done_ref.shape[0]
    copies = []

    def send(where, row):
        copy = pltpu.make_async_copy(where, to_ref.at[pl.ds(row, size)], sem.at[len(copies)])
        copy.start()
        copies.append(copy)

    for row in range(0, done, size):
        send(done_ref.at[pl.ds(row, size)], row)
    for row in range(0, last.shape[0], size):
        for start in range(0, last.shape[1], COLS):
            last[row : row + size, start : start + COLS] = (
                total_ref[row : row + size, start : start + COLS]
                + jnp.dot(
                    a_ref[row : row + size], b_ref[:, start : start + COLS], preferred_element_type=jnp.float32
                )
            ).astype(last.dtype)
        send(last.at[pl.ds(row, size)], done + row)
    for copy in copies:
        copy.wait()


def shards(amplitudes, pair_mask, integrals):
    rows, width = amplitudes.shape
    depth, columns = integrals.shape
    deep = depth * 2 * RING * RING
    chunks = rows // CHUNK
    dma = pltpu.SemaphoreType.DMA
    held = pl.pallas_call(
        kernel,
        out_shape=[
            jax.ShapeDtypeStruct((rows - REST, columns), jnp.bfloat16),
            jax.ShapeDtypeStruct((REST, columns), jnp.float32),
            jax.ShapeDtypeStruct((REST, CORES * width), jnp.bfloat16),
            jax.ShapeDtypeStruct((CORES * width, columns), jnp.bfloat16),
        ],
        in_specs=[
            pl.BlockSpec(memory_space=pltpu.HBM),
            pl.BlockSpec(memory_space=pltpu.HBM),
            pl.BlockSpec(memory_space=pltpu.HBM),
        ],
        out_specs=[pl.BlockSpec(memory_space=pltpu.VMEM)] * 4,
        scratch_shapes=[
            pltpu.SMEM((1, rows // VB), jnp.int32),
            pltpu.VMEM((rows, width), jnp.bfloat16),
            pltpu.VMEM((LINE, CORES, rows, width), jnp.bfloat16),
            pltpu.VMEM((deep, columns), jnp.bfloat16),
            pltpu.VMEM((rows - REST, columns), jnp.float32),
            dma((3,)),
            dma((LINE, chunks)),
            dma((LINE, chunks)),
            dma((LINE,)),
            dma((LINE,)),
            dma((LINE,)),
            dma((2, RING, RING, 2)),
            dma((1,)),
            pltpu.SemaphoreType.REGULAR((3,)),
        ],
        compiler_params=pltpu.CompilerParams(
            collective_id=0, has_side_effects=True, vmem_limit_bytes=40 * 2**20
        ),
        cost_estimate=pl.CostEstimate(
            flops=2 * rows * columns * deep, bytes_accessed=2 * rows * columns, transcendentals=0
        ),
    )(*[pltpu.with_memory_space_constraint(v, pltpu.HBM) for v in (pair_mask.reshape(1, -1), amplitudes, integrals)])
    return pl.pallas_call(
        finish_rows,
        out_shape=jax.ShapeDtypeStruct((rows, columns), jnp.bfloat16),
        in_specs=[pl.BlockSpec(memory_space=pltpu.VMEM)] * 4,
        out_specs=pl.BlockSpec(memory_space=pltpu.HBM),
        scratch_shapes=[pltpu.VMEM((REST, columns), jnp.bfloat16), dma((rows // BLOCK,))],
        compiler_params=pltpu.CompilerParams(vmem_limit_bytes=20 * 2**20),
        cost_estimate=pl.CostEstimate(
            flops=2 * REST * columns * CORES * width, bytes_accessed=2 * rows * columns, transcendentals=0
        ),
    )(*held)


def solution(mesh):
    placed = P("wide", "narrow")
    return jax.shard_map(
        shards, mesh=mesh, in_specs=(placed, placed, placed), out_specs=placed, check_vma=False
    )
```

```python
import functools

import jax
import jax.numpy as jnp
from jax import lax
from jax.experimental import pallas as pl
from jax.experimental.pallas import tpu as pltpu
from jax.sharding import PartitionSpec as P

MESH = pl.DeviceIdType.MESH
VB = 128
LINE = 4
RING = 4
CORES = 2
CHUNK = 256
BLOCK = 256
TALL = 512
REST = 1024
AHEAD = 3
COLS = 512


def kernel(
    mask_hbm,
    a_ref,
    b_ref,
    out_ref,
    total_rest,
    a_rest,
    b_rest,
    mask_ref,
    a_in,
    a_all,
    b_all,
    total,
    local,
    za,
    ca,
    up,
    down,
    side,
    zb,
    sb,
    ready,
):
    wide, narrow = lax.axis_index("wide"), lax.axis_index("narrow")
    zl, core = narrow // CORES, narrow % CORES
    x, zh, y = wide // (2 * RING), (wide // RING) % 2, wide % RING
    rows, width = a_in.shape
    depth = b_ref.shape[0]
    half = depth // 2
    chunks = rows // CHUNK
    near = jnp.where(zl < LINE // 2, 0, LINE // 2)
    middle = jnp.where(zl < LINE // 2, LINE // 2, LINE // 2 - 1)
    late = jnp.where(zl < LINE // 2, LINE - 1, 0)

    def wide_of(layer, first, second):
        px = (x + (1 - core) * first + core * second) % RING
        py = (y + core * first + (1 - core) * second) % RING
        return (px * 2 + (zh + layer) % 2) * RING + py

    other = (wide, zl * CORES + 1 - core)
    above, below = (wide, narrow + CORES), (wide, narrow - CORES)

    take_b = pltpu.make_async_copy(b_ref, b_all.at[pl.ds(wide * depth, depth)], local.at[0])
    take_a = pltpu.make_async_copy(a_ref, a_in, local.at[1])
    take_mask = pltpu.make_async_copy(mask_hbm, mask_ref, local.at[2])
    take_a.start()
    take_mask.start()
    take_b.start()

    barrier = pltpu.get_barrier_semaphore()

    def greet(device):
        pl.semaphore_signal(barrier, inc=1, device_id=device, device_id_type=MESH)

    peer = (wide_of(1, 0, 0), narrow)

    def to_x(px):
        return (((px + RING) % RING * 2 + zh) * RING + y, narrow)

    def to_y(py):
        return ((x * 2 + zh) * RING + (py + RING) % RING, narrow)

    higher = (
        (x < RING - 1, to_x(x + 1), 1),
        (x == 0, to_x(RING - 1), 1),
        (y < RING - 1, to_y(y + 1), 1),
        (y == 0, to_y(RING - 1), 1),
        (zl < LINE - 1, above, 0),
        (zh == 0, peer, 2),
    )
    lower = (
        (x > 0, to_x(x - 1), 1),
        (x == RING - 1, to_x(0), 1),
        (y > 0, to_y(y - 1), 1),
        (y == RING - 1, to_y(0), 1),
        (zl > 0, below, 0),
        (zh == 1, peer, 2),
    )
    greet(other)
    for present, device, _ in higher:
        pl.when(present)(functools.partial(greet, device))

    def count(*conditions):
        return sum(jnp.where(c, 1, 0) for c in conditions)

    before = count(*(present for present, _, _ in lower))
    pl.semaphore_wait(barrier, 1 + before)
    for present, device, kind in lower:
        pl.when(present)(
            functools.partial(
                pl.semaphore_signal, ready.at[kind], inc=1, device_id=device, device_id_type=MESH
            )
        )
    inner = jnp.where((zl > 0) & (zl < LINE - 1), 1, 0)
    in_plane = count(*(present for present, _, kind in higher if kind == 1))


    def b_part(layer, first, second, part):
        base = wide_of(layer, first, second) * depth
        if part is None:
            return b_all.at[pl.ds(base, depth)]
        return b_all.at[pl.ds(base + part * half, half)]

    def b_copy(layer, first, second, part, to, label):
        where = b_part(layer, first, second, part)
        return pltpu.make_async_remote_copy(
            where,
            where,
            sb.at[0],
            zb.at[label[0], label[1] % RING, label[2] % RING, part or 0],
            device_id=(wide_of(*to), narrow),
            device_id_type=MESH,
        )

    def b_send(layer, first, second, part, step):
        df, ds = step
        b_copy(layer, first, second, part, (0, df, ds), (layer, first - df, second - ds)).start()

    def b_wait(layer, first, second, part):
        where = b_part(layer, first, second, part)
        pltpu.make_async_remote_copy(
            where,
            where,
            sb.at[0],
            zb.at[layer, first % RING, second % RING, part or 0],
            device_id=other,
            device_id_type=MESH,
        ).wait_recv()

    def b_both(layer, first, part):
        b_send(layer, first, 0, part, (0, 1))
        b_send(layer, first, 0, part, (0, 3))

    def b_begin(layer, part):
        b_send(layer, 0, 0, part, (1, 0))
        b_send(layer, 0, 0, part, (3, 0))
        b_both(layer, 0, part)

    def b_near(layer, part):
        ahead, behind = ((3, 1), (1, 3))[part]
        b_wait(layer, ahead, 0, part)
        b_send(layer, ahead, 0, part, (behind, 0))
        b_both(layer, ahead, part)
        b_wait(layer, behind, 0, part)
        b_both(layer, behind, part)

    def b_far(layer, part):
        b_wait(layer, 2, 0, part)
        b_both(layer, 2, part)

    def b_turn(layer, first):
        b_wait(layer, first, 3, 0)
        b_send(layer, first, 3, 0, (0, 1))
        b_wait(layer, first, 1, 1)
        b_send(layer, first, 1, 1, (0, 3))

    def b_end(layer):
        for first in range(RING):
            b_wait(layer, first, 3, 1)
            b_wait(layer, first, 1, 0)
            b_wait(layer, first, 2, 0)
            b_wait(layer, first, 2, 1)

    swaps = [b_copy(0, 0, 0, part, (1, 0, 0), (1, 0, 0)) for part in (0, 1)]
    take_b.wait()

    @pl.when(zh == 1)
    def _():
        for swap in swaps:
            swap.start()

    def a_copy(source, r, send, recv, device):
        where = a_all.at[source, core, pl.ds(pl.multiple_of(r * CHUNK, CHUNK), CHUNK)]
        return pltpu.make_async_remote_copy(
            where, where, send.at[source], recv, device_id=device, device_id_type=MESH
        )

    def over(source, r):
        return a_copy(source, r, side, ca.at[source, jnp.where(source == late, r, 0)], other)

    def upward(source, r):
        return a_copy(source, r, up, za.at[source, r], above)

    def downward(source, r):
        return a_copy(source, r, down, za.at[source, r], below)

    def from_other(where, r, source):
        pltpu.make_async_remote_copy(
            where, where, side.at[source], ca.at[source, r], device_id=other, device_id_type=MESH
        ).wait_recv()

    take_a.wait()
    take_mask.wait()

    def own(r, _):
        for i in range(CHUNK // VB):
            at = r * (CHUNK // VB) + i
            span = pl.ds(pl.multiple_of(at * VB, VB), VB)
            keep = mask_ref[0, at].astype(jnp.float32)
            a_all[zl, core, span, :] = (a_in[span, :].astype(jnp.float32) * keep).astype(jnp.bfloat16)

        @pl.when(zl > 0)
        def _():
            downward(zl, r).start()

        over(zl, r).start()
        return 0

    def own_up(r, _):
        upward(zl, r).start()
        return 0

    def own_ups(start, stop):
        @pl.when(zl < LINE - 1)
        def _():
            lax.fori_loop(start, stop, own_up, 0)

    ahead = jnp.where(inner == 0, AHEAD, jnp.where(zl == LINE // 2, 2 * AHEAD, chunks))
    held_back = jnp.where(zh == 0, ahead, chunks)
    lax.fori_loop(0, held_back, own, 0)

    @pl.when(zl < LINE - 1)
    def _():
        pl.semaphore_wait(ready.at[0], 1)

    own_ups(0, held_back)

    @pl.when(in_plane > 0)
    def _():
        pl.semaphore_wait(ready.at[1], in_plane)

    b_begin(0, 0)
    b_begin(0, 1)

    def forward(distance, r):
        @pl.when(zl - distance >= 0)
        def _():
            upward(zl - distance, r).wait_recv()

            @pl.when(zl < LINE - 1)
            def _():
                upward(zl - distance, r).start()

            over(zl - distance, r).start()

        @pl.when(zl + distance < LINE)
        def _():
            downward(zl + distance, r).wait_recv()

            @pl.when(zl > 0)
            def _():
                downward(zl + distance, r).start()

            over(zl + distance, r).start()

    def forwards(distance, start, stop):
        def body(r, _):
            forward(distance, r)
            return 0

        lax.fori_loop(start * chunks // 16, stop * chunks // 16, body, 0)

    def tile(place, c, span):
        return a_all[place, c, span, :]

    def deep(place, c):
        return pl.ds(pl.multiple_of((place * CORES + c) * width, width), width)

    def multiply(places, span, start):
        left = jnp.concatenate([tile(place, c, span) for place, c in places], axis=1)
        right = jnp.concatenate([b_all[deep(place, c), start : start + COLS] for place, c in places], axis=0)
        return jnp.dot(left, right, preferred_element_type=jnp.float32)

    columns = out_ref.shape[1]
    talls = total.shape[0] // TALL
    rest_talls = REST // TALL

    def first_part(q, into, skip):
        span = pl.ds(pl.multiple_of((q + skip) * TALL, TALL), TALL)
        here = pl.ds(pl.multiple_of(q * TALL, TALL), TALL)
        for start in range(0, columns, COLS):
            into[here, start : start + COLS] = multiply([(near, zh), (near + 1, zh)], span, start)

    def second_part(q, into, skip):
        span = pl.ds(pl.multiple_of((q + skip) * TALL, TALL), TALL)
        here = pl.ds(pl.multiple_of(q * TALL, TALL), TALL)
        places = [(near, 1 - zh), (near + 1, 1 - zh), (middle, 0), (middle, 1)]
        for start in range(0, columns, COLS):
            into[here, start : start + COLS] += multiply(places, span, start)

    def parts(part, distance, first_chunk, last_chunk):
        per = (last_chunk - first_chunk) // (talls + rest_talls)

        def body(q, _):
            part(q, total, 0)
            for i in range(per):
                forward(distance, first_chunk + q * per + i)
            return 0

        def rest_body(q, _):
            part(q, total_rest, talls)
            for i in range(per):
                forward(distance, first_chunk + (talls + q) * per + i)
            return 0

        lax.fori_loop(0, talls, body, 0)
        lax.fori_loop(0, rest_talls, rest_body, 0)

    def slice_of(q):
        if q < talls:
            first_part(q, total, 0)
        else:
            first_part(q - talls, total_rest, talls)

    b_near(0, 0)
    b_near(0, 1)
    b_turn(0, 0)

    @pl.when(zh == 0)
    def _():
        pl.semaphore_wait(ready.at[2], 1)
        for swap in swaps:
            swap.start()

    lax.fori_loop(held_back, chunks, own, 0)
    own_ups(held_back, chunks)
    b_far(0, 0)
    b_far(0, 1)
    b_turn(0, 3)
    forwards(1, 0, 6)
    b_turn(0, 1)
    forwards(1, 6, 10)
    b_turn(0, 2)
    forwards(1, 10, 12)
    b_wait(1, 0, 0, 0)
    b_begin(1, 0)
    forwards(1, 12, 14)
    b_wait(1, 0, 0, 1)
    b_begin(1, 1)
    b_near(1, 0)
    forwards(1, 14, 16)
    b_near(1, 1)
    b_end(0)
    for i in range(2):
        from_other(a_all.at[near + i, 1 - core], 0, near + i)
    b_far(1, 0)
    slice_of(0)
    b_turn(1, 0)
    b_far(1, 1)
    slice_of(1)
    forwards(2, 0, 2)
    b_turn(1, 3)
    slice_of(2)
    forwards(2, 2, 5)
    b_turn(1, 1)
    slice_of(3)
    forwards(2, 5, 8)
    b_turn(1, 2)
    forwards(2, 8, 16)
    b_end(1)
    from_other(a_all.at[middle, 1 - core], 0, middle)
    b_rest[...] = b_all[pl.ds(pl.multiple_of(late * CORES * width, CORES * width), CORES * width)]
    parts(second_part, 3, 0, chunks // 2)

    def arrive(start, stop):
        def body(r, _):
            from_other(a_all.at[late, 1 - core, pl.ds(pl.multiple_of(r * CHUNK, CHUNK), CHUNK)], r, late)
            return 0

        lax.fori_loop(start, stop, body, 0)

    def final(q):
        span = pl.ds(pl.multiple_of(q * BLOCK, BLOCK), BLOCK)
        for start in range(0, columns, COLS):
            out_ref[span, start : start + COLS] = (
                total[span, start : start + COLS] + multiply([(late, 0), (late, 1)], span, start)
            ).astype(out_ref.dtype)

    blocks = total.shape[0] // BLOCK
    per = BLOCK // CHUNK

    def last_part(q, _):
        forward(3, chunks // 2 + q)
        arrive(q * per, (q + 1) * per)
        final(q)
        return 0

    lax.fori_loop(0, blocks, last_part, 0)

    def last_forward(r, _):
        forward(3, r)
        return 0

    lax.fori_loop(chunks // 2 + blocks, chunks, last_forward, 0)
    arrive(blocks * per, chunks)
    for c in range(CORES):
        a_rest[:, c * width : (c + 1) * width] = a_all[late, c, pl.ds(rows - REST, REST), :]

    everything = b_all.at[pl.ds(0, b_all.shape[0] - depth)]
    pltpu.make_async_remote_copy(
        everything, everything, sb.at[0], zb.at[0, 0, 0, 0], device_id=other, device_id_type=MESH
    ).wait_send()

    def finish(source, _):
        def sent(sem):
            where = a_all.at[source, core]
            pltpu.make_async_remote_copy(
                where, where, sem.at[source], za.at[0, 0], device_id=other, device_id_type=MESH
            ).wait_send()

        sent(side)

        @pl.when((source <= zl) & (zl < LINE - 1))
        def _():
            sent(up)

        @pl.when((source >= zl) & (zl > 0))
        def _():
            sent(down)

        return 0

    lax.fori_loop(0, LINE, finish, 0)


def finish_rows(done_ref, total_ref, a_ref, b_ref, to_ref, last, sem):
    size, done = BLOCK, done_ref.shape[0]
    copies = []

    def send(where, row):
        copy = pltpu.make_async_copy(where, to_ref.at[pl.ds(row, size)], sem.at[len(copies)])
        copy.start()
        copies.append(copy)

    for row in range(0, done, size):
        send(done_ref.at[pl.ds(row, size)], row)
    for row in range(0, last.shape[0], size):
        for start in range(0, last.shape[1], COLS):
            last[row : row + size, start : start + COLS] = (
                total_ref[row : row + size, start : start + COLS]
                + jnp.dot(
                    a_ref[row : row + size], b_ref[:, start : start + COLS], preferred_element_type=jnp.float32
                )
            ).astype(last.dtype)
        send(last.at[pl.ds(row, size)], done + row)
    for copy in copies:
        copy.wait()


def shards(amplitudes, pair_mask, integrals):
    rows, width = amplitudes.shape
    depth, columns = integrals.shape
    deep = depth * 2 * RING * RING
    chunks = rows // CHUNK
    dma = pltpu.SemaphoreType.DMA
    held = pl.pallas_call(
        kernel,
        out_shape=[
            jax.ShapeDtypeStruct((rows - REST, columns), jnp.bfloat16),
            jax.ShapeDtypeStruct((REST, columns), jnp.float32),
            jax.ShapeDtypeStruct((REST, CORES * width), jnp.bfloat16),
            jax.ShapeDtypeStruct((CORES * width, columns), jnp.bfloat16),
        ],
        in_specs=[
            pl.BlockSpec(memory_space=pltpu.HBM),
            pl.BlockSpec(memory_space=pltpu.HBM),
            pl.BlockSpec(memory_space=pltpu.HBM),
        ],
        out_specs=[pl.BlockSpec(memory_space=pltpu.VMEM)] * 4,
        scratch_shapes=[
            pltpu.SMEM((1, rows // VB), jnp.int32),
            pltpu.VMEM((rows, width), jnp.bfloat16),
            pltpu.VMEM((LINE, CORES, rows, width), jnp.bfloat16),
            pltpu.VMEM((deep, columns), jnp.bfloat16),
            pltpu.VMEM((rows - REST, columns), jnp.float32),
            dma((3,)),
            dma((LINE, chunks)),
            dma((LINE, chunks)),
            dma((LINE,)),
            dma((LINE,)),
            dma((LINE,)),
            dma((2, RING, RING, 2)),
            dma((1,)),
            pltpu.SemaphoreType.REGULAR((3,)),
        ],
        compiler_params=pltpu.CompilerParams(
            collective_id=0, has_side_effects=True, vmem_limit_bytes=40 * 2**20
        ),
        cost_estimate=pl.CostEstimate(
            flops=2 * rows * columns * deep, bytes_accessed=2 * rows * columns, transcendentals=0
        ),
    )(*[pltpu.with_memory_space_constraint(v, pltpu.HBM) for v in (pair_mask.reshape(1, -1), amplitudes, integrals)])
    return pl.pallas_call(
        finish_rows,
        out_shape=jax.ShapeDtypeStruct((rows, columns), jnp.bfloat16),
        in_specs=[pl.BlockSpec(memory_space=pltpu.VMEM)] * 4,
        out_specs=pl.BlockSpec(memory_space=pltpu.HBM),
        scratch_shapes=[pltpu.VMEM((REST, columns), jnp.bfloat16), dma((rows // BLOCK,))],
        compiler_params=pltpu.CompilerParams(vmem_limit_bytes=20 * 2**20),
        cost_estimate=pl.CostEstimate(
            flops=2 * REST * columns * CORES * width, bytes_accessed=2 * rows * columns, transcendentals=0
        ),
    )(*held)


def solution(mesh):
    placed = P("wide", "narrow")
    return jax.shard_map(
        shards, mesh=mesh, in_specs=(placed, placed, placed), out_specs=placed, check_vma=False
    )
```
